128 devices in a mesh: lat: 8 (over y, core), wave: 16 (over z, x).
Axes of the slice: x: 4, y: 4, z: 4, core: 2. Of those that a mesh axis runs over, the one named last changes fastest.
Arguments:
- grid_field: bfloat16 [2, 512, 64, 2048], P(None, 'lat', 'wave'), may hold values from -6 to 6
- points: int32 [512], P('lat'), may hold values from 16 to 2048, as said below
- weights: float32 [512], P('lat'), may hold values from 0.5 to 2
- owners: int32 [256], replicated, may hold values from 0 to 255, as said below
- legendre: bfloat16 [256, 2, 512, 512], P('wave'), may hold values from -0.0805 to 0.0805, as said below
- spectral_variance: float32 [64, 1024], P('lat'), may hold values from 0.1 to 1
- vertical: bfloat16 [64, 64], replicated, may hold values from -0.305 to 1.81
Outputs:
- smoothed: bfloat16 [2, 512, 64, 2048], P(None, 'lat', 'wave')
The draws below stay inside these ranges and needn't reach their ends.
Inputs may be any that keep to these rules, and one draw needn't show every extreme that they name: `owners`: every wavenumber appears once. Owner w along wave holds slots w * 16 to (w+1) * 16 - 1; slots 2t and 2t+1 hold m and 255 - m. Never falling from the pole toward the equator; the row nearest the equator has exactly 2048 points. legendre[r, q, k, i] is zero where 2k+q < owners[r].
All inputs are finite; a program needn't handle non-finite values.
Results may differ from the reference program's by a relative error of at most 0.014.
Values may be sent and summed in bfloat16 or wider, within the bound.
No kernel may reach another device: no remote copies, remote signals or barrier semaphores. Data moves between devices by JAX's collectives and lax.ppermute only.
A program may use at most 192 MiB of HBM per device.

```python
import math
import jax
import jax.numpy as jnp
from jax import lax

HLAT = 512
LONMAX = 2048
M = 256
NT = 1024
LEV = 64


def owner_pairs(key):
    pair_order = jax.random.permutation(key, M // 2).astype(jnp.int32)
    return jnp.stack([pair_order, M - 1 - pair_order], axis=1).reshape(M)


def draw_owners(key, part):
    return owner_pairs(key)


def draw_legendre(key, part):
    owners = owner_pairs(key)
    key = jax.random.fold_in(key, 7)
    values = jax.random.uniform(key, (M, 2, NT // 2, HLAT), jnp.float32, -0.08, 0.08)
    degree = 2 * jnp.arange(NT // 2, dtype=jnp.int32)[None, :] + jnp.arange(2, dtype=jnp.int32)[:, None]
    nonzero = degree[None, :, :, None] >= owners[:, None, None, None]
    return jnp.where(nonzero, values, 0.0).astype(jnp.bfloat16)


def draw_points(key, part):
    key = jax.random.fold_in(key, 11)
    spacing = 16 + 4 * jnp.arange(HLAT, dtype=jnp.int32) + jax.random.randint(key, (HLAT,), 0, 4, jnp.int32)
    spacing = jnp.minimum(spacing, LONMAX)
    return spacing.at[HLAT - 1].set(LONMAX)


def draw_vertical(key, part):
    key = jax.random.fold_in(key, 13)
    identity = jnp.eye(LEV, dtype=jnp.float32)
    noise_part = jax.random.uniform(key, (LEV, LEV), jnp.float32, -0.3, 0.3)
    return (1.5 * identity + noise_part).astype(jnp.bfloat16)


def shard_levels(stream_key, dims, shards, smallest, high):
    def one(axis_at, parts):
        heights = jax.random.uniform(jax.random.fold_in(jax.random.fold_in(stream_key, 6), axis_at), (parts,), jnp.float32, smallest / len(shards), high / len(shards))
        return jnp.repeat(jnp.exp(heights), dims[axis_at] // parts).reshape((-1,) + (1,) * (len(dims) - axis_at - 1))

    gain = one(*shards[0])
    for cut in shards[1:]:
        gain = gain * one(*cut)
    return gain


def bell_draw(stream_key, shape, scale, bound, cuts=(), kind=jnp.bfloat16):
    result = scale * jax.random.normal(stream_key, shape, jnp.float32)
    if cuts:
        result = result * shard_levels(stream_key, shape, cuts, -0.22, 0.18)
    return jnp.clip(result, -bound, bound).astype(kind)


def setup_inputs(seed: int = 0) -> dict:
    arg_keys = jax.random.split(jax.random.key(seed), 8)
    grid_field = bell_draw(arg_keys[0], (2, HLAT, LEV, LONMAX), 1.0, 6.0, ((1, 8), (2, 16)))
    points = draw_points(jax.random.fold_in(arg_keys[7], 71), 0)
    weights = jnp.clip(jnp.exp(math.log(2.0) - 1.3862944 * jax.random.uniform(arg_keys[2], (HLAT,), jnp.float32) ** shard_levels(arg_keys[2], (HLAT,), ((0, 8),), -0.2, 0.2)), 0.5, 2.0)
    owners = draw_owners(jax.random.fold_in(arg_keys[7], 71), 0)
    legendre = draw_legendre(jax.random.fold_in(arg_keys[7], 71), 0)
    spectral_variance = jnp.clip(jnp.exp(math.log(1.0) - 2.3025851 * jax.random.uniform(arg_keys[5], (LEV, NT), jnp.float32) ** shard_levels(arg_keys[5], (LEV, NT), ((0, 8),), -0.2, 0.2)), 0.1, 1.0)
    vertical = draw_vertical(jax.random.fold_in(arg_keys[7], 71), 0)
    return {"grid_field": grid_field, "points": points, "weights": weights, "owners": owners, "legendre": legendre, "spectral_variance": spectral_variance, "vertical": vertical}


def fourier_factors(row_points, owners, longitudes):
    column_index = jnp.arange(longitudes, dtype=jnp.int32)
    phase_index = (owners[None, :] * column_index[:, None]) % row_points
    angles = phase_index.astype(jnp.float32) * (2.0 * math.pi) / row_points.astype(jnp.float32)
    inside = (column_index[:, None] < row_points) & (2 * owners[None, :] < row_points)
    inside = jnp.concatenate([inside, inside], axis=1)
    factors = jnp.concatenate([jnp.cos(angles), -jnp.sin(angles)], axis=1)
    return jnp.where(inside, factors, 0.0).astype(jnp.bfloat16)


def reference(grid_field, points, weights, owners, legendre, spectral_variance, vertical):
    slot_count = owners.shape[0]

    def analyse(row_index):
        row_points = points[row_index]
        factors = fourier_factors(row_points, owners, LONMAX).astype(jnp.float32)
        row_values = lax.dynamic_index_in_dim(grid_field, row_index, 1, keepdims=False)
        spectrum = jnp.dot(row_values.reshape(2 * LEV, LONMAX).astype(jnp.float32), factors)
        spectrum = spectrum * (weights[row_index] / row_points.astype(jnp.float32))
        spectrum = spectrum.reshape(2, LEV, 2, slot_count)
        return jnp.stack([spectrum[0] + spectrum[1], spectrum[0] - spectrum[1]], axis=0)

    folded = lax.map(analyse, jnp.arange(HLAT, dtype=jnp.int32))
    folded = jnp.transpose(folded, (4, 1, 3, 2, 0)).astype(jnp.bfloat16)
    vertical_full = vertical.astype(jnp.float32)
    mixed_levels = jnp.einsum('msclh,lo->mscoh', folded.astype(jnp.float32), vertical_full).astype(jnp.bfloat16)
    parity = owners % 2
    spread = spectral_variance.reshape(LEV, NT // 2, 2).transpose(2, 0, 1)

    def transform(slot):
        values_table, values, odd_wave = slot
        values_table = values_table.astype(jnp.float32)
        paired = values.reshape(2, 2 * LEV, HLAT).astype(jnp.float32)
        even_rows = jnp.where(odd_wave == 0, paired[0], paired[1])
        odd_rows = jnp.where(odd_wave == 1, paired[0], paired[1])
        operand = jnp.stack([even_rows, odd_rows], axis=0)
        coefficient = jnp.einsum('qkl,qcl->qck', values_table, operand)
        scaled = (coefficient.reshape(2, 2, LEV, NT // 2) * spread[:, None, :, :]).astype(jnp.bfloat16)
        scaled = scaled.reshape(2, 2 * LEV, NT // 2).astype(jnp.float32)
        synthesis = jnp.einsum('qkl,qck->qcl', values_table, scaled)
        symmetric = jnp.where(odd_wave == 0, synthesis[0], synthesis[1])
        antisym = jnp.where(odd_wave == 0, synthesis[1], synthesis[0])
        return jnp.stack([symmetric, antisym], axis=0).reshape(2, 2, LEV, HLAT).astype(jnp.bfloat16)

    returned = lax.map(transform, (legendre, mixed_levels, parity))
    remixed = jnp.einsum('msclh,ol->mscoh', returned.astype(jnp.float32), vertical_full).astype(jnp.bfloat16)
    remixed = remixed.astype(jnp.float32)
    unfolded = jnp.stack([remixed[:, 0] + remixed[:, 1], remixed[:, 0] - remixed[:, 1]], axis=0).astype(jnp.bfloat16)
    per_row = jnp.transpose(unfolded, (4, 0, 3, 2, 1))
    doubling = jnp.where(owners == 0, 1.0, 2.0).astype(jnp.bfloat16)
    doubling = jnp.concatenate([doubling, doubling])

    def synthesise(row_index):
        row_points = points[row_index]
        factors = (fourier_factors(row_points, owners, LONMAX) * doubling).astype(jnp.float32)
        coefs_row = lax.dynamic_index_in_dim(per_row, row_index, 0, keepdims=False)
        coefs_row = coefs_row.reshape(2 * LEV, 2 * slot_count).astype(jnp.float32)
        gridded = jnp.dot(coefs_row, factors.T)
        return gridded.reshape(2, LEV, LONMAX).astype(jnp.bfloat16)

    result_rows = lax.map(synthesise, jnp.arange(HLAT, dtype=jnp.int32))
    return jnp.transpose(result_rows, (1, 0, 2, 3))
```

```python
import functools

import jax
import jax.numpy as jnp
import numpy as np
from jax import lax
from jax.experimental import pallas as pl
from jax.experimental.pallas import tpu as pltpu
from jax.sharding import PartitionSpec as P

ROWS = 8
CHUNK = 128
BUILT = 3
VMEM_LIMIT = 56 * 1024 * 1024

SIN_TERMS = (3.141592640130707, -5.167710083507862, 2.550077523214134, -0.5982912856178576, 0.0776576603009221)
COS_TERMS = (0.9999999532476082, -4.93479283061961, 4.058411352862034, -1.3318765680776314, 0.2196896110917421)


def polynomial(terms, square):
    total = jnp.full_like(square, terms[-1])
    for term in terms[-2::-1]:
        total = total * square + term
    return total


def phasor(product, length, inverse):
    turns = jnp.floor(product * inverse + 0.5)
    part = (product - turns * length) * inverse
    square = part * part
    sine = part * polynomial(SIN_TERMS, square)
    cosine = polynomial(COS_TERMS, square)
    return 1.0 - 2.0 * sine * sine, 2.0 * sine * cosine


def multiply(a, b):
    return a[0] * b[0] - a[1] * b[1], a[0] * b[1] + a[1] * b[0]


def square(a):
    return a[0] * a[0] - a[1] * a[1], 2.0 * a[0] * a[1]


def times_transposed(a, b):
    return lax.dot_general(a, b, (((1,), (1,)), ((), ())), preferred_element_type=jnp.float32)


def lengths_by_row(points_ref, first, shape):
    row = lax.broadcasted_iota(jnp.int32, shape, 0)
    lengths = jnp.zeros(shape, jnp.int32)
    for r in range(ROWS):
        lengths = jnp.where(row == r, points_ref[first + r], lengths)
    lengths = lengths.astype(jnp.float32)
    return lengths, 1.0 / lengths


def place_phasors(step_ref, waves, lengths, inverse):
    cosine, sine = phasor(waves, lengths, inverse)
    turn, at = (cosine, -sine), 1
    keep = {1: 0, 2: 2, 4: 4, 8: 6, CHUNK: 10, 2 * CHUNK: 12}
    while True:
        if at in keep:
            step_ref[keep[at]], step_ref[keep[at] + 1] = turn
        if at in (8, 16, 2 * CHUNK):
            step_ref[{8: 8, 16: 9, 2 * CHUNK: 14}[at]] = 2.0 * turn[0]
        if at == 2 * CHUNK:
            break
        turn, at = square(turn), 2 * at


def swap_sublanes(values):
    values = list(values)
    sublane = lax.broadcasted_iota(jnp.int32, values[0].shape, 0)
    for d in (4, 2, 1):
        low = sublane & d == 0
        for a in range(8):
            if a & d == 0:
                first, second = values[a], values[a + d]
                values[a] = jnp.where(low, first, pltpu.roll(second, d, 0))
                values[a + d] = jnp.where(low, pltpu.roll(first, 8 - d, 0), second)
    return values


def steps_of(step_ref, which, r):
    slots = step_ref.shape[2]
    return tuple(jnp.broadcast_to(step_ref[n, r:r + 1, :], (8, slots)) for n in which)


def build_table(table_ref, step_ref, r):
    slots = step_ref.shape[2]
    size = table_ref.shape[0]
    sublane = lax.broadcasted_iota(jnp.int32, (8, slots), 0)
    powers = []
    for n in range(3):
        power = steps_of(step_ref, (2 * n, 2 * n + 1), r)
        powers.append(tuple(jnp.where(sublane & (1 << n) == 0, 1.0 - c, power[c]) for c in range(2)))
    real, imaginary, twice, twice_next = steps_of(step_ref, (6, 7, 8, 9), r)
    values = [multiply(multiply(powers[0], powers[1]), powers[2])]
    values.append(multiply(values[0], (real, imaginary)))
    for n in range(2, size // 8):
        if n < 4:
            values.append(tuple(twice * values[n - 1][c] - values[n - 2][c] for c in range(2)))
        else:
            values.append(tuple(twice_next * values[n - 2][c] - values[n - 4][c] for c in range(2)))
        if n % 2:
            for c in range(2):
                both = jnp.concatenate([values[n - 1][c], values[n][c]], axis=0).astype(jnp.bfloat16)
                table_ref[8 * n - 8:8 * n + 8, c * slots:(c + 1) * slots] = both
        elif n == 2:
            for c in range(2):
                both = jnp.concatenate([values[0][c], values[1][c]], axis=0).astype(jnp.bfloat16)
                table_ref[:16, c * slots:(c + 1) * slots] = both


def analysis_kernel(order, points_ref, weights_ref, wave_ref, owners_ref, variance_ref, field_ref, out_ref,
                    phasors_ref, own_ref, step_ref, table_ref, rows_ref, sums_ref, order_ref, sems, phasor_sems):
    slots = owners_ref.shape[1]
    tiles = [slice(t, t + 128) for t in range(0, slots, 128)]
    rows, height = own_ref.shape[1:3]

    def arrival(g):
        at = pl.ds(g * ROWS, ROWS)
        return pltpu.make_async_copy(field_ref.at[:, at], own_ref.at[:, at], sems.at[g])

    def departure(g):
        at = pl.ds(pl.multiple_of(g * ROWS, ROWS), ROWS)
        return pltpu.make_async_copy(step_ref.at[:, at], phasors_ref.at[:, at], phasor_sems.at[g])

    for g in range(rows // ROWS):
        arrival(g).start()
    waves = jnp.broadcast_to(owners_ref[...].astype(jnp.float32), (ROWS, slots))
    sublane = lax.broadcasted_iota(jnp.int32, (8, slots), 0)
    position = lax.broadcasted_iota(jnp.int32, (height, CHUNK), 0) // 4 * CHUNK
    position = position + lax.broadcasted_iota(jnp.int32, (height, CHUNK), 1)

    def group(g, _):
        first = g * ROWS
        lengths, inverse = lengths_by_row(points_ref, first, (ROWS, slots))
        here = step_ref.at[:, pl.ds(pl.multiple_of(first, ROWS), ROWS)]
        place_phasors(here, waves, lengths, inverse)
        departure(g).start()
        arrival(g).wait()
        for r in range(ROWS):
            length = points_ref[first + r]

            build_table(table_ref.at[r], here, r)
            inside = jnp.where(position < length, 1.0, 0.0).astype(jnp.bfloat16)
            points = jnp.concatenate([own_ref[0, first + r] * inside, own_ref[1, first + r] * inside], axis=0)
            parts = jnp.dot(points, table_ref[r], preferred_element_type=jnp.float32)
            chunk, pair, twice = steps_of(here, (10, 11), r), steps_of(here, (12, 13), r), steps_of(here, (14,), r)[0]
            sums = []
            for h in range(2):
                blocks = [
                    tuple(parts[b:b + 8, c * slots:(c + 1) * slots] for c in range(2))
                    for b in range(h * height, (h + 1) * height, 8)
                ]
                later, total = blocks[-1], tuple(blocks[-2][c] + twice * blocks[-1][c] for c in range(2))
                for part in blocks[-3:0:-1]:
                    later, total = total, tuple(part[c] + (twice * total[c] - later[c]) for c in range(2))
                total = multiply(total, pair)
                sums.append(tuple(total[c] + (blocks[0][c] - later[c]) for c in range(2)))
            scale = weights_ref[first + r] / length.astype(jnp.float32)
            scale = jnp.where(2 * owners_ref[...] < length, scale, 0.0)
            firsts, seconds = [], []
            for c in range(2):
                added, taken = sums[0][c] + sums[1][c], sums[0][c] - sums[1][c]
                firsts.append(jnp.where(sublane < 4, added, pltpu.roll(taken, 4, 0)))
                seconds.append(jnp.where(sublane < 4, pltpu.roll(added, 4, 0), taken))
            seconds = multiply(seconds, chunk)
            for c in range(2):
                rows_ref[c, r] = (firsts[c] + seconds[c]) * scale
        for c in range(2):
            for t, lanes in enumerate(tiles):
                for row, part in enumerate(swap_sublanes([rows_ref[c, r, :, lanes] for r in range(ROWS)])):
                    sums_ref[t, row, pl.ds(pl.multiple_of(c * 64 + first, 8), 8), :] = part
        return 0

    lax.fori_loop(0, rows // ROWS, group, 0)

    for row in range(8):
        for t in range(len(tiles)):
            order_ref[t, row] = sums_ref[t, row].T
    variance = variance_ref[...]
    variance = jnp.where(wave_ref[0] % 2 == 1, pltpu.roll(variance, 64, 1), variance)
    upper = variance.astype(jnp.bfloat16).astype(jnp.float32)
    lane = lax.broadcasted_iota(jnp.int32, variance.shape, 1)
    variance = jnp.where(lane < 64, upper, pltpu.roll(variance - upper, 64, 1)).astype(jnp.bfloat16)
    where = {t: n for n, t in enumerate(order)}
    for slot in range(0, slots, 8):
        at = slice(slot % 128, slot % 128 + 8)
        parts = swap_sublanes([order_ref[slot // 128, row, at, :] for row in range(8)])
        for n in range(0, 8, 2):
            to = where[(slot + n) // 2]
            out_ref[to, :16] = jnp.concatenate(parts[n:n + 2], axis=0).astype(jnp.bfloat16)
            out_ref[to, 16:] = variance
    for g in range(rows // ROWS):
        departure(g).wait()


def matrices_of(made_ref):
    size = made_ref.shape[1]
    return made_ref.at[:size], made_ref.at[size:2 * size], made_ref.at[2 * size:]


def place_matrices(vertical_ref, mix_in_ref, mix_out_ref, parting_ref):
    levels = vertical_ref.shape[0]
    vertical = vertical_ref[...].astype(jnp.float32)
    index = lax.broadcasted_iota(jnp.int32, (4 * levels, levels), 0)
    level = lax.broadcasted_iota(jnp.int32, (4 * levels, levels), 1)
    by_block = jnp.where(level == index // 16 * 4 + index % 4, 1.0, 0.0)
    by_slot = jnp.where(level == index % levels, 1.0, 0.0)
    row = lax.broadcasted_iota(jnp.int32, (4 * levels, 4 * levels), 0)
    col = lax.broadcasted_iota(jnp.int32, (4 * levels, 4 * levels), 1)
    by_rows = jnp.dot(by_block, vertical, preferred_element_type=jnp.float32)
    mix_in = times_transposed(by_slot, by_rows)
    mix_in_ref[...] = jnp.where(row // levels == col % 16 // 4, mix_in, 0.0).astype(jnp.bfloat16)
    mix_out = times_transposed(by_rows, by_slot)
    sign = jnp.where((row % 8 // 4 == 1) & (col // levels % 2 == 1), -1.0, 1.0)
    mix_out_ref[...] = jnp.where(row % 16 // 8 == col // (2 * levels), mix_out * sign, 0.0).astype(jnp.bfloat16)
    degree = lax.broadcasted_iota(jnp.int32, parting_ref.shape, 0)
    degree = degree // 128 * 64 + degree % 64
    lane = lax.broadcasted_iota(jnp.int32, parting_ref.shape, 1)
    parting_ref[...] = jnp.where(degree == 2 * (lane % 128) + lane // 128, 1.0, 0.0).astype(jnp.bfloat16)


def table_kernel(step_ref, vertical_ref, out_ref, made_ref, pairs_ref, table_ref, sems):
    groups = step_ref.shape[1] // ROWS - BUILT

    def departure(g):
        at = pl.ds(g * (ROWS // 2), ROWS // 2)
        return pltpu.make_async_copy(pairs_ref.at[at], out_ref.at[at], sems.at[g])

    def group(g, _):
        here = step_ref.at[:, pl.ds(pl.multiple_of((g + BUILT) * ROWS, ROWS), ROWS)]
        for r in range(ROWS):
            build_table(table_ref.at[r], here, r)
            pairs_ref[g * (ROWS // 2) + r // 2, :, (r % 2) * CHUNK:(r % 2 + 1) * CHUNK] = table_ref[r].T
        departure(g).start()
        return 0

    lax.fori_loop(0, groups, group, 0)
    place_matrices(vertical_ref, *matrices_of(made_ref))
    for g in range(groups):
        departure(g).wait()


def synthesis_kernel(order, points_ref, owners_ref, values_ref, far_table_ref, turns_ref, out_ref,
                     own_ref, table_ref, built_ref, order_ref, coefs_ref, table_sems, sems):
    slots = owners_ref.shape[1]
    tiles = [slice(t, t + 128) for t in range(0, slots, 128)]
    rows, height = own_ref.shape[1:3]

    def arrival(g):
        at = pl.ds(g * (ROWS // 2), ROWS // 2)
        return pltpu.make_async_copy(far_table_ref.at[at], table_ref.at[at], table_sems.at[g])

    def departure(g):
        at = pl.ds(g * ROWS, ROWS)
        return pltpu.make_async_copy(own_ref.at[:, at], out_ref.at[:, at], sems.at[g])

    for g in range(rows // ROWS - BUILT):
        arrival(g).start()
    where = {t: n for n, t in enumerate(order)}
    for slot in range(0, slots, 8):
        parts = []
        for n in range(0, 8, 2):
            pair = values_ref[where[(slot + n) // 2]].astype(jnp.float32)
            parts += [pair[:8], pair[8:]]
        for row, part in enumerate(swap_sublanes(parts)):
            order_ref[slot // 128, row, slot % 128:slot % 128 + 8, :] = part
    for t in range(len(tiles)):
        for row in range(8):
            order_ref[t, row] = order_ref[t, row].T
        for n in range(0, 128, 8):
            parts = swap_sublanes([order_ref[t, row, n:n + 8, :] for row in range(8)])
            for at, part in enumerate(parts):
                coefs_ref[t, n + at] = part

    doubling = jnp.where(owners_ref[...] == 0, 1.0, 2.0)
    sublane = lax.broadcasted_iota(jnp.int32, (8, slots), 0)
    position = lax.broadcasted_iota(jnp.int32, (height, CHUNK), 0) // 4 * CHUNK
    position = position + lax.broadcasted_iota(jnp.int32, (height, CHUNK), 1)

    def group(g, built):
        first = g * ROWS
        if built:
            here = turns_ref.at[:, pl.ds(pl.multiple_of(first, ROWS), ROWS)]
        else:
            arrival(g - BUILT).wait()
        for r in range(ROWS):
            row = first + r
            length = points_ref[row]
            turns = [jnp.broadcast_to(turns_ref[n, pl.ds(row, 1), :], (8, slots)) for n in range(10, 15)]
            chunk, pair, twice = (turns[0], -turns[1]), (turns[2], -turns[3]), turns[4]
            scale = jnp.where(2 * owners_ref[...] < length, doubling, 0.0)
            start = tuple(jnp.where(sublane < 4, 1.0 - c, chunk[c]) * scale for c in range(2))
            values = [
                [coefs_ref[t, c * 64 + row] for t in range(len(tiles))]
                for c in range(2)
            ]
            values = [jnp.concatenate(part, axis=1) for part in values]
            others = [pltpu.roll(part, 4, 0) for part in values]
            turned = []
            for low, high in ((values, others), (others, values)):
                before = multiply(start, [jnp.where(sublane < 4, low[c], high[c]) for c in range(2)])
                value = multiply(before, pair)
                turned += [jnp.concatenate(before, axis=1), jnp.concatenate(value, axis=1)]
                for _ in range(2, height // 8):
                    before, value = value, tuple(twice * value[c] - before[c] for c in range(2))
                    turned.append(jnp.concatenate(value, axis=1))
            turned = jnp.concatenate(turned, axis=0).astype(jnp.bfloat16)
            if built:
                build_table(built_ref.at[r], here, r)
                gridded = times_transposed(turned, built_ref[r])
            else:
                table = table_ref[(g - BUILT) * (ROWS // 2) + r // 2, :, (r % 2) * CHUNK:(r % 2 + 1) * CHUNK]
                gridded = jnp.dot(turned, table, preferred_element_type=jnp.float32)
            for h in range(2):
                own_ref[h, row] = jnp.where(
                    position < length, gridded[h * height:(h + 1) * height], 0.0
                ).astype(jnp.bfloat16)
        departure(g).start()

    for start, end, built in ((0, BUILT, True), (BUILT, rows // ROWS, False)):
        lax.fori_loop(start, end, lambda g, _, built=built: (group(g, built), 0)[1], 0)
    for g in range(rows // ROWS):
        departure(g).wait()


def swap_halves(first, second):
    low = lax.broadcasted_iota(jnp.int32, first.shape, 1) < 64
    return (
        jnp.where(low, first, pltpu.roll(second, 64, 1)),
        jnp.where(low, pltpu.roll(first, 64, 1), second),
    )


def spectral_kernel(order, place_ref, values_ref, legendre_ref, made_ref, out_ref,
                    mixed_ref, back_ref, own_ref, sems):
    levels = made_ref.shape[1] // 4
    copies = {}
    for slot in range(2):
        for q in range(2):
            copies[slot, q] = pltpu.make_async_copy(
                legendre_ref.at[place_ref[0] + slot, q], own_ref.at[slot, q], sems.at[slot, q]
            )
            copies[slot, q].start()
    mix_in, mix_out, parting = (part[...] for part in matrices_of(made_ref))
    where = {t: n for n, t in enumerate(order)}
    for p in range(4):
        bands = [
            jnp.concatenate([values_ref[where[w * 8 + v], :16] for w in range(16)], axis=0)
            for v in (2 * p, 2 * p + 1)
        ]
        mixed = jnp.dot(mix_in, jnp.concatenate(bands, axis=1), preferred_element_type=jnp.float32)
        for c, part in enumerate(swap_halves(mixed[:, :128], mixed[:, 128:])):
            part = part.astype(jnp.bfloat16)
            for k in range(4):
                mixed_ref[k, c * levels:(c + 1) * levels, p * 128:(p + 1) * 128] = (
                    part[k * levels:(k + 1) * levels]
                )
    halves = [
        jnp.concatenate([values_ref[where[w * 8 + v], 16:].astype(jnp.float32) for v in range(8)], axis=0)
        for w in range(16)
    ]
    halves = jnp.concatenate([jnp.concatenate(halves[n:n + 4], axis=1) for n in range(0, 16, 4)], axis=0)
    parted = jnp.dot(halves.astype(jnp.bfloat16), parting, preferred_element_type=jnp.float32)
    parted = [parted[n * levels:(n + 1) * levels] for n in range(4)]
    spreads = [jnp.concatenate([part[:, q * 128:(q + 1) * 128] for part in parted], axis=1) for q in range(2)]
    for slot in range(2):
        parity = place_ref[1 + slot]
        for q in range(2):
            s = (q + parity) % 2
            copies[slot, q].wait()
            values = own_ref[slot, q]
            coefficient = times_transposed(mixed_ref[2 * slot + s], values)
            spread = spreads[q]
            scaled = coefficient * jnp.concatenate([spread, spread], axis=0)
            back_ref[2 * slot + s] = jnp.dot(
                scaled.astype(jnp.bfloat16), values, preferred_element_type=jnp.float32
            )
    for p in range(4):
        lanes = slice(p * 128, (p + 1) * 128)
        halves = [
            jnp.concatenate([back_ref[k, c * levels:(c + 1) * levels, lanes] for k in range(4)], axis=0)
            for c in range(2)
        ]
        parts = jnp.concatenate(swap_halves(*halves), axis=1).astype(jnp.bfloat16)
        remixed = jnp.dot(mix_out, parts, preferred_element_type=jnp.float32).astype(jnp.bfloat16)
        for n in range(2):
            for w in range(16):
                out_ref[where[w * 8 + 2 * p + n]] = remixed[16 * w:16 * w + 16, n * 128:(n + 1) * 128]


def local(grid_field, points, weights, owners, legendre, spectral_variance, vertical):
    _, band_rows, few_levels, longitudes = grid_field.shape
    slots = owners.shape[0]
    levels = vertical.shape[0]
    half_degree, rows = legendre.shape[2:]
    wave, lat = lax.axis_index("wave"), lax.axis_index("lat")
    own = owners.reshape(1, slots)
    parities = lax.dynamic_slice_in_dim(owners, 2 * (wave * lax.axis_size("lat") + lat), 2, 0) % 2
    place = jnp.concatenate([(2 * lat).reshape(1), parities])
    params = pltpu.CompilerParams(vmem_limit_bytes=VMEM_LIMIT)

    order = [int(t) for t in np.random.RandomState(5).permutation(slots // 2)]
    exchange = functools.partial(
        lax.all_to_all, axis_name=("wave", "lat"), split_axis=0, concat_axis=0, axis_index_groups=[order], tiled=True
    )

    chunks = longitudes // CHUNK
    height = chunks * few_levels
    field = grid_field.reshape(2, band_rows, few_levels, chunks, CHUNK).transpose(0, 1, 3, 2, 4)
    field = field.reshape(2, band_rows, height, CHUNK)
    own_spec = pl.BlockSpec((1, slots), lambda g, *_: (0, 0))
    regroup_scratch = [
        pltpu.VMEM((slots // 128, 8, 128, 128), jnp.float32),
        pltpu.VMEM((slots // 128, 8, 128, 128), jnp.float32),
    ]

    far = pl.BlockSpec(memory_space=pltpu.HBM)
    made_shape = (16 * levels, 4 * levels)

    def matrix_spec(shape):
        return pl.BlockSpec(shape, lambda g, *_: (0, 0))

    def blocks_spec(height):
        return pl.BlockSpec((slots // 2, height, 128), lambda g, *_: (0, 0, 0))

    sums, phasors = pl.pallas_call(
        functools.partial(analysis_kernel, order),
        grid_spec=pltpu.PrefetchScalarGridSpec(
            num_scalar_prefetch=3,
            grid=(1,),
            in_specs=[
                own_spec,
                pl.BlockSpec((spectral_variance.shape[0], 128), lambda g, p, w, wave: (0, wave[0] // 2)),
                far,
            ],
            out_specs=[blocks_spec(24), far],
            scratch_shapes=[
                pltpu.VMEM(field.shape, jnp.bfloat16),
                pltpu.VMEM((15, band_rows, slots), jnp.float32),
                pltpu.VMEM((ROWS, CHUNK, 2 * slots), jnp.bfloat16),
                pltpu.VMEM((2, ROWS, 8, slots), jnp.float32),
            ] + regroup_scratch + [
                pltpu.SemaphoreType.DMA((band_rows // ROWS,)),
                pltpu.SemaphoreType.DMA((band_rows // ROWS,)),
            ],
        ),
        out_shape=[
            jax.ShapeDtypeStruct((slots // 2, 24, 128), jnp.bfloat16),
            jax.ShapeDtypeStruct((15, band_rows, slots), jnp.float32),
        ],
        compiler_params=params,
        name="analysis",
    )(points, weights, wave.reshape(1), own, spectral_variance, field)

    arrived = exchange(sums)

    phasors_spec = pl.BlockSpec((15, band_rows, slots), lambda g, *_: (0, 0, 0))
    table_shape = (band_rows // 2 - BUILT * (ROWS // 2), 2 * slots, 2 * CHUNK)
    table, made = pl.pallas_call(
        table_kernel,
        grid=(1,),
        in_specs=[phasors_spec, matrix_spec((levels, levels))],
        out_specs=[far, matrix_spec(made_shape)],
        scratch_shapes=[
            pltpu.VMEM(table_shape, jnp.bfloat16),
            pltpu.VMEM((ROWS, CHUNK, 2 * slots), jnp.bfloat16),
            pltpu.SemaphoreType.DMA((band_rows // ROWS - BUILT,)),
        ],
        out_shape=[
            jax.ShapeDtypeStruct(table_shape, jnp.bfloat16),
            jax.ShapeDtypeStruct(made_shape, jnp.bfloat16),
        ],
        compiler_params=pltpu.CompilerParams(vmem_limit_bytes=50 * 1024 * 1024),
        cost_estimate=pl.CostEstimate(flops=8 * 10**9, bytes_accessed=9 * 10**6, transcendentals=0),
        name="tables",
    )(phasors, vertical)

    remixed = pl.pallas_call(
        functools.partial(spectral_kernel, order),
        grid_spec=pltpu.PrefetchScalarGridSpec(
            num_scalar_prefetch=1,
            grid=(1,),
            in_specs=[blocks_spec(24), far, matrix_spec(made_shape)],
            out_specs=blocks_spec(16),
            scratch_shapes=[
                pltpu.VMEM((4, 2 * levels, rows), jnp.bfloat16),
                pltpu.VMEM((4, 2 * levels, rows), jnp.float32),
                pltpu.VMEM((2, 2, half_degree, rows), jnp.bfloat16),
                pltpu.SemaphoreType.DMA((2, 2)),
            ],
        ),
        out_shape=jax.ShapeDtypeStruct((slots // 2, 16, 128), jnp.bfloat16),
        compiler_params=pltpu.CompilerParams(vmem_limit_bytes=50 * 1024 * 1024),
        name="spectral",
    )(place, arrived, legendre, made)

    returned = exchange(remixed)

    smoothed = pl.pallas_call(
        functools.partial(synthesis_kernel, order),
        grid_spec=pltpu.PrefetchScalarGridSpec(
            num_scalar_prefetch=1,
            grid=(1,),
            in_specs=[own_spec, blocks_spec(16), far, phasors_spec],
            out_specs=far,
            scratch_shapes=[
                pltpu.VMEM(field.shape, jnp.bfloat16),
                pltpu.VMEM(table_shape, jnp.bfloat16),
                pltpu.VMEM((ROWS, CHUNK, 2 * slots), jnp.bfloat16),
                pltpu.VMEM((slots // 128, 8, 128, 128), jnp.float32),
                pltpu.VMEM((slots // 128, 128, 8, 128), jnp.float32),
                pltpu.SemaphoreType.DMA((band_rows // ROWS - BUILT,)),
                pltpu.SemaphoreType.DMA((band_rows // ROWS,)),
            ],
        ),
        out_shape=jax.ShapeDtypeStruct(field.shape, jnp.bfloat16),
        compiler_params=pltpu.CompilerParams(vmem_limit_bytes=50 * 1024 * 1024),
        name="synthesis",
    )(points, own, returned, table, phasors)
    smoothed = smoothed.reshape(2, band_rows, chunks, few_levels, CHUNK).transpose(0, 1, 3, 2, 4)
    return smoothed.reshape(grid_field.shape)


def solution(mesh):
    return jax.shard_map(
        local,
        mesh=mesh,
        in_specs=(
            P(None, "lat", "wave", None),
            P("lat"),
            P("lat"),
            P(),
            P("wave", None, None, None),
            P("lat", None),
            P(),
        ),
        out_specs=P(None, "lat", "wave", None),
        check_vma=False,
    )
```

```python
import functools

import jax
import jax.numpy as jnp
import numpy as np
from jax import lax
from jax.experimental import pallas as pl
from jax.experimental.pallas import tpu as pltpu
from jax.sharding import PartitionSpec as P

ROWS = 8
CHUNK = 128
APART = 1024
BUILT = 2
VMEM_LIMIT = 56 * 1024 * 1024

SIN_TERMS = (3.141592640130707, -5.167710083507862, 2.550077523214134, -0.5982912856178576, 0.0776576603009221)
COS_TERMS = (0.9999999532476082, -4.93479283061961, 4.058411352862034, -1.3318765680776314, 0.2196896110917421)


def polynomial(terms, square):
    total = jnp.full_like(square, terms[-1])
    for term in terms[-2::-1]:
        total = total * square + term
    return total


def phasor(product, length, inverse):
    turns = jnp.floor(product * inverse + 0.5)
    part = (product - turns * length) * inverse
    square = part * part
    sine = part * polynomial(SIN_TERMS, square)
    cosine = polynomial(COS_TERMS, square)
    return 1.0 - 2.0 * sine * sine, 2.0 * sine * cosine


def multiply(a, b):
    return a[0] * b[0] - a[1] * b[1], a[0] * b[1] + a[1] * b[0]


def square(a):
    return a[0] * a[0] - a[1] * a[1], 2.0 * a[0] * a[1]


def times_transposed(a, b):
    return lax.dot_general(a, b, (((1,), (1,)), ((), ())), preferred_element_type=jnp.float32)


def lengths_by_row(points_ref, first, shape):
    row = lax.broadcasted_iota(jnp.int32, shape, 0)
    lengths = jnp.zeros(shape, jnp.int32)
    for r in range(ROWS):
        lengths = jnp.where(row == r, points_ref[first + r], lengths)
    lengths = lengths.astype(jnp.float32)
    return lengths, 1.0 / lengths


def place_phasors(step_ref, waves, lengths, inverse):
    cosine, sine = phasor(waves, lengths, inverse)
    turn, at = (cosine, -sine), 1
    keep = {1: 0, 2: 2, 4: 4, 8: 6, CHUNK: 10, 2 * CHUNK: 12, APART: 15}
    while True:
        if at in keep:
            step_ref[keep[at]], step_ref[keep[at] + 1] = turn
        if at in (8, 16, 2 * CHUNK):
            step_ref[{8: 8, 16: 9, 2 * CHUNK: 14}[at]] = 2.0 * turn[0]
        if at == APART:
            break
        turn, at = square(turn), 2 * at


def swap_sublanes(values):
    values = list(values)
    sublane = lax.broadcasted_iota(jnp.int32, values[0].shape, 0)
    for d in (4, 2, 1):
        low = sublane & d == 0
        for a in range(8):
            if a & d == 0:
                first, second = values[a], values[a + d]
                values[a] = jnp.where(low, first, pltpu.roll(second, d, 0))
                values[a + d] = jnp.where(low, pltpu.roll(first, 8 - d, 0), second)
    return values


def steps_of(step_ref, which, r):
    slots = step_ref.shape[2]
    return tuple(jnp.broadcast_to(step_ref[n, r:r + 1, :], (8, slots)) for n in which)


def build_table(table_ref, step_ref, r):
    slots = step_ref.shape[2]
    size = table_ref.shape[0]
    sublane = lax.broadcasted_iota(jnp.int32, (8, slots), 0)
    powers = []
    for n in range(3):
        power = steps_of(step_ref, (2 * n, 2 * n + 1), r)
        powers.append(tuple(jnp.where(sublane & (1 << n) == 0, 1.0 - c, power[c]) for c in range(2)))
    real, imaginary, twice, twice_next = steps_of(step_ref, (6, 7, 8, 9), r)
    values = [multiply(multiply(powers[0], powers[1]), powers[2])]
    values.append(multiply(values[0], (real, imaginary)))
    for top in range(0, table_ref.shape[0], CHUNK):
        if top:
            values = [multiply(value, steps_of(step_ref, (15, 16), r)) for value in values[:2]]
        for n in range(2, CHUNK // 8 + 2):
            if n % 2 == 0:
                for c in range(2):
                    both = jnp.concatenate([values[n - 2][c], values[n - 1][c]], axis=0).astype(jnp.bfloat16)
                    table_ref[top + 8 * n - 16:top + 8 * n, c * slots:(c + 1) * slots] = both
            if n < 4:
                values.append(tuple(twice * values[n - 1][c] - values[n - 2][c] for c in range(2)))
            elif n < CHUNK // 8:
                values.append(tuple(twice_next * values[n - 2][c] - values[n - 4][c] for c in range(2)))


def analysis_kernel(order, points_ref, weights_ref, wave_ref, owners_ref, variance_ref, field_ref, out_ref,
                    phasors_ref, own_ref, step_ref, table_ref, rows_ref, sums_ref, order_ref, sems, phasor_sems):
    slots = owners_ref.shape[1]
    tiles = [slice(t, t + 128) for t in range(0, slots, 128)]
    rows, height = own_ref.shape[1:3]

    def arrival(g):
        at = pl.ds(g * ROWS, ROWS)
        return pltpu.make_async_copy(field_ref.at[:, at], own_ref.at[:, at], sems.at[g])

    def departure(g):
        at = pl.ds(pl.multiple_of(g * ROWS, ROWS), ROWS)
        return pltpu.make_async_copy(step_ref.at[:15, at], phasors_ref.at[:, at], phasor_sems.at[g])

    for g in range(rows // ROWS):
        arrival(g).start()
    waves = jnp.broadcast_to(owners_ref[...].astype(jnp.float32), (ROWS, slots))
    sublane = lax.broadcasted_iota(jnp.int32, (8, slots), 0)
    position = lax.broadcasted_iota(jnp.int32, (height, CHUNK), 0) // 4 * CHUNK
    position = position + lax.broadcasted_iota(jnp.int32, (height, CHUNK), 1)
    half = height // 2
    position = jnp.concatenate([position[:half], position[half:]], axis=1)

    def group(g, _):
        first = g * ROWS
        lengths, inverse = lengths_by_row(points_ref, first, (ROWS, slots))
        here = step_ref.at[:, pl.ds(pl.multiple_of(first, ROWS), ROWS)]
        place_phasors(here, waves, lengths, inverse)
        departure(g).start()
        arrival(g).wait()
        for r in range(ROWS):
            length = points_ref[first + r]

            build_table(table_ref.at[r], here, r)
            inside = jnp.where(position < length, 1.0, 0.0).astype(jnp.bfloat16)
            points = [
                jnp.concatenate([own_ref[n, first + r, :half, :], own_ref[n, first + r, half:, :]], axis=1) * inside
                for n in range(2)
            ]
            points = jnp.concatenate(points, axis=0)
            parts = jnp.dot(points, table_ref[r], preferred_element_type=jnp.float32)
            chunk, pair, twice = steps_of(here, (10, 11), r), steps_of(here, (12, 13), r), steps_of(here, (14,), r)[0]
            sums = []
            for h in range(2):
                blocks = [
                    tuple(parts[b:b + 8, c * slots:(c + 1) * slots] for c in range(2))
                    for b in range(h * half, (h + 1) * half, 8)
                ]
                later, total = blocks[-1], tuple(blocks[-2][c] + twice * blocks[-1][c] for c in range(2))
                for part in blocks[-3:0:-1]:
                    later, total = total, tuple(part[c] + (twice * total[c] - later[c]) for c in range(2))
                total = multiply(total, pair)
                sums.append(tuple(total[c] + (blocks[0][c] - later[c]) for c in range(2)))
            scale = weights_ref[first + r] / length.astype(jnp.float32)
            scale = jnp.where(2 * owners_ref[...] < length, scale, 0.0)
            firsts, seconds = [], []
            for c in range(2):
                added, taken = sums[0][c] + sums[1][c], sums[0][c] - sums[1][c]
                firsts.append(jnp.where(sublane < 4, added, pltpu.roll(taken, 4, 0)))
                seconds.append(jnp.where(sublane < 4, pltpu.roll(added, 4, 0), taken))
            seconds = multiply(seconds, chunk)
            for c in range(2):
                rows_ref[c, r] = (firsts[c] + seconds[c]) * scale
        for c in range(2):
            for t, lanes in enumerate(tiles):
                for row, part in enumerate(swap_sublanes([rows_ref[c, r, :, lanes] for r in range(ROWS)])):
                    sums_ref[t, row, pl.ds(pl.multiple_of(c * 64 + first, 8), 8), :] = part
        return 0

    lax.fori_loop(0, rows // ROWS, group, 0)

    for row in range(8):
        for t in range(len(tiles)):
            order_ref[t, row] = sums_ref[t, row].T
    variance = variance_ref[...]
    variance = jnp.where(wave_ref[0] % 2 == 1, pltpu.roll(variance, 64, 1), variance)
    upper = variance.astype(jnp.bfloat16).astype(jnp.float32)
    lane = lax.broadcasted_iota(jnp.int32, variance.shape, 1)
    variance = jnp.where(lane < 64, upper, pltpu.roll(variance - upper, 64, 1)).astype(jnp.bfloat16)
    where = {t: n for n, t in enumerate(order)}
    for slot in range(0, slots, 8):
        at = slice(slot % 128, slot % 128 + 8)
        parts = swap_sublanes([order_ref[slot // 128, row, at, :] for row in range(8)])
        for n in range(0, 8, 2):
            to = where[(slot + n) // 2]
            out_ref[to, :16] = jnp.concatenate(parts[n:n + 2], axis=0).astype(jnp.bfloat16)
            out_ref[to, 16:] = variance
    for g in range(rows // ROWS):
        departure(g).wait()


def matrices_of(made_ref):
    size = made_ref.shape[1]
    return made_ref.at[:size], made_ref.at[size:2 * size], made_ref.at[2 * size:]


def place_matrices(vertical_ref, mix_in_ref, mix_out_ref, parting_ref):
    levels = vertical_ref.shape[0]
    vertical = vertical_ref[...].astype(jnp.float32)
    index = lax.broadcasted_iota(jnp.int32, (4 * levels, levels), 0)
    level = lax.broadcasted_iota(jnp.int32, (4 * levels, levels), 1)
    by_block = jnp.where(level == index // 16 * 4 + index % 4, 1.0, 0.0)
    by_slot = jnp.where(level == index % levels, 1.0, 0.0)
    row = lax.broadcasted_iota(jnp.int32, (4 * levels, 4 * levels), 0)
    col = lax.broadcasted_iota(jnp.int32, (4 * levels, 4 * levels), 1)
    by_rows = jnp.dot(by_block, vertical, preferred_element_type=jnp.float32)
    mix_in = times_transposed(by_slot, by_rows)
    mix_in_ref[...] = jnp.where(row // levels == col % 16 // 4, mix_in, 0.0).astype(jnp.bfloat16)
    mix_out = times_transposed(by_rows, by_slot)
    sign = jnp.where((row % 8 // 4 == 1) & (col // levels % 2 == 1), -1.0, 1.0)
    mix_out_ref[...] = jnp.where(row % 16 // 8 == col // (2 * levels), mix_out * sign, 0.0).astype(jnp.bfloat16)
    degree = lax.broadcasted_iota(jnp.int32, parting_ref.shape, 0)
    degree = degree // 128 * 64 + degree % 64
    lane = lax.broadcasted_iota(jnp.int32, parting_ref.shape, 1)
    parting_ref[...] = jnp.where(degree == 2 * (lane % 128) + lane // 128, 1.0, 0.0).astype(jnp.bfloat16)


def table_kernel(step_ref, vertical_ref, out_ref, made_ref, pairs_ref, table_ref, sems):
    groups = step_ref.shape[1] // ROWS - BUILT

    def departure(g):
        at = pl.ds(g * (ROWS // 2), ROWS // 2)
        return pltpu.make_async_copy(pairs_ref.at[at], out_ref.at[at], sems.at[g])

    def group(g, _):
        here = step_ref.at[:, pl.ds(pl.multiple_of((g + BUILT) * ROWS, ROWS), ROWS)]
        for r in range(ROWS):
            build_table(table_ref.at[r], here, r)
            pairs_ref[g * (ROWS // 2) + r // 2, :, (r % 2) * CHUNK:(r % 2 + 1) * CHUNK] = table_ref[r].T
        departure(g).start()
        return 0

    lax.fori_loop(0, groups, group, 0)
    place_matrices(vertical_ref, *matrices_of(made_ref))
    for g in range(groups):
        departure(g).wait()


def synthesis_kernel(order, points_ref, owners_ref, values_ref, far_table_ref, turns_ref, out_ref,
                     own_ref, table_ref, built_ref, order_ref, coefs_ref, table_sems, sems):
    slots = owners_ref.shape[1]
    tiles = [slice(t, t + 128) for t in range(0, slots, 128)]
    rows, height = own_ref.shape[1:3]

    def arrival(g):
        at = pl.ds(g * (ROWS // 2), ROWS // 2)
        return pltpu.make_async_copy(far_table_ref.at[at], table_ref.at[at], table_sems.at[g])

    def departure(g):
        at = pl.ds(g * ROWS, ROWS)
        return pltpu.make_async_copy(own_ref.at[:, at], out_ref.at[:, at], sems.at[g])

    for g in range(rows // ROWS - BUILT):
        arrival(g).start()
    where = {t: n for n, t in enumerate(order)}
    for slot in range(0, slots, 8):
        parts = []
        for n in range(0, 8, 2):
            pair = values_ref[where[(slot + n) // 2]].astype(jnp.float32)
            parts += [pair[:8], pair[8:]]
        for row, part in enumerate(swap_sublanes(parts)):
            order_ref[slot // 128, row, slot % 128:slot % 128 + 8, :] = part
    for t in range(len(tiles)):
        for row in range(8):
            order_ref[t, row] = order_ref[t, row].T
        for n in range(0, 128, 8):
            parts = swap_sublanes([order_ref[t, row, n:n + 8, :] for row in range(8)])
            for at, part in enumerate(parts):
                coefs_ref[t, n + at] = part

    doubling = jnp.where(owners_ref[...] == 0, 1.0, 2.0)
    sublane = lax.broadcasted_iota(jnp.int32, (8, slots), 0)
    position = lax.broadcasted_iota(jnp.int32, (height, CHUNK), 0) // 4 * CHUNK
    position = position + lax.broadcasted_iota(jnp.int32, (height, CHUNK), 1)

    def group(g, built):
        first = g * ROWS
        if built:
            here = turns_ref.at[:, pl.ds(pl.multiple_of(first, ROWS), ROWS)]
        else:
            arrival(g - BUILT).wait()
        for r in range(ROWS):
            row = first + r
            length = points_ref[row]
            turns = [jnp.broadcast_to(turns_ref[n, pl.ds(row, 1), :], (8, slots)) for n in range(10, 15)]
            chunk, pair, twice = (turns[0], -turns[1]), (turns[2], -turns[3]), turns[4]
            scale = jnp.where(2 * owners_ref[...] < length, doubling, 0.0)
            start = tuple(jnp.where(sublane < 4, 1.0 - c, chunk[c]) * scale for c in range(2))
            values = [
                [coefs_ref[t, c * 64 + row] for t in range(len(tiles))]
                for c in range(2)
            ]
            values = [jnp.concatenate(part, axis=1) for part in values]
            others = [pltpu.roll(part, 4, 0) for part in values]
            turned = []
            for low, high in ((values, others), (others, values)):
                before = multiply(start, [jnp.where(sublane < 4, low[c], high[c]) for c in range(2)])
                value = multiply(before, pair)
                turned += [jnp.concatenate(before, axis=1), jnp.concatenate(value, axis=1)]
                for _ in range(2, height // 8):
                    before, value = value, tuple(twice * value[c] - before[c] for c in range(2))
                    turned.append(jnp.concatenate(value, axis=1))
            turned = jnp.concatenate(turned, axis=0).astype(jnp.bfloat16)
            if built:
                build_table(built_ref.at[r], here, r)
                gridded = times_transposed(turned, built_ref[r])
            else:
                table = table_ref[(g - BUILT) * (ROWS // 2) + r // 2, :, (r % 2) * CHUNK:(r % 2 + 1) * CHUNK]
                gridded = jnp.dot(turned, table, preferred_element_type=jnp.float32)
            for h in range(2):
                own_ref[h, row] = jnp.where(
                    position < length, gridded[h * height:(h + 1) * height], 0.0
                ).astype(jnp.bfloat16)
        departure(g).start()

    for start, end, built in ((0, BUILT, True), (BUILT, rows // ROWS, False)):
        lax.fori_loop(start, end, lambda g, _, built=built: (group(g, built), 0)[1], 0)
    for g in range(rows // ROWS):
        departure(g).wait()


def swap_halves(first, second):
    low = lax.broadcasted_iota(jnp.int32, first.shape, 1) < 64
    return (
        jnp.where(low, first, pltpu.roll(second, 64, 1)),
        jnp.where(low, pltpu.roll(first, 64, 1), second),
    )


def spectral_kernel(order, place_ref, values_ref, legendre_ref, made_ref, out_ref,
                    mixed_ref, back_ref, own_ref, sems):
    levels = made_ref.shape[1] // 4
    copies = {}
    for slot in range(2):
        for q in range(2):
            copies[slot, q] = pltpu.make_async_copy(
                legendre_ref.at[place_ref[0] + slot, q], own_ref.at[slot, q], sems.at[slot, q]
            )
            copies[slot, q].start()
    mix_in, mix_out, parting = (part[...] for part in matrices_of(made_ref))
    where = {t: n for n, t in enumerate(order)}
    for p in range(4):
        bands = [
            jnp.concatenate([values_ref[where[w * 8 + v], :16] for w in range(16)], axis=0)
            for v in (2 * p, 2 * p + 1)
        ]
        mixed = jnp.dot(mix_in, jnp.concatenate(bands, axis=1), preferred_element_type=jnp.float32)
        for c, part in enumerate(swap_halves(mixed[:, :128], mixed[:, 128:])):
            part = part.astype(jnp.bfloat16)
            for k in range(4):
                mixed_ref[k, c * levels:(c + 1) * levels, p * 128:(p + 1) * 128] = (
                    part[k * levels:(k + 1) * levels]
                )
    halves = [
        jnp.concatenate([values_ref[where[w * 8 + v], 16:].astype(jnp.float32) for v in range(8)], axis=0)
        for w in range(16)
    ]
    halves = jnp.concatenate([jnp.concatenate(halves[n:n + 4], axis=1) for n in range(0, 16, 4)], axis=0)
    parted = jnp.dot(halves.astype(jnp.bfloat16), parting, preferred_element_type=jnp.float32)
    parted = [parted[n * levels:(n + 1) * levels] for n in range(4)]
    spreads = [jnp.concatenate([part[:, q * 128:(q + 1) * 128] for part in parted], axis=1) for q in range(2)]
    for slot in range(2):
        parity = place_ref[1 + slot]
        for q in range(2):
            s = (q + parity) % 2
            copies[slot, q].wait()
            values = own_ref[slot, q]
            coefficient = times_transposed(mixed_ref[2 * slot + s], values)
            spread = spreads[q]
            scaled = coefficient * jnp.concatenate([spread, spread], axis=0)
            back_ref[2 * slot + s] = jnp.dot(
                scaled.astype(jnp.bfloat16), values, preferred_element_type=jnp.float32
            )
    for p in range(4):
        lanes = slice(p * 128, (p + 1) * 128)
        halves = [
            jnp.concatenate([back_ref[k, c * levels:(c + 1) * levels, lanes] for k in range(4)], axis=0)
            for c in range(2)
        ]
        parts = jnp.concatenate(swap_halves(*halves), axis=1).astype(jnp.bfloat16)
        remixed = jnp.dot(mix_out, parts, preferred_element_type=jnp.float32).astype(jnp.bfloat16)
        for n in range(2):
            for w in range(16):
                out_ref[where[w * 8 + 2 * p + n]] = remixed[16 * w:16 * w + 16, n * 128:(n + 1) * 128]


def local(grid_field, points, weights, owners, legendre, spectral_variance, vertical):
    _, band_rows, few_levels, longitudes = grid_field.shape
    slots = owners.shape[0]
    levels = vertical.shape[0]
    half_degree, rows = legendre.shape[2:]
    wave, lat = lax.axis_index("wave"), lax.axis_index("lat")
    own = owners.reshape(1, slots)
    parities = lax.dynamic_slice_in_dim(owners, 2 * (wave * lax.axis_size("lat") + lat), 2, 0) % 2
    place = jnp.concatenate([(2 * lat).reshape(1), parities])
    params = pltpu.CompilerParams(vmem_limit_bytes=VMEM_LIMIT)

    order = [int(t) for t in np.random.RandomState(5).permutation(slots // 2)]
    exchange = functools.partial(
        lax.all_to_all, axis_name=("wave", "lat"), split_axis=0, concat_axis=0, axis_index_groups=[order], tiled=True
    )

    chunks = longitudes // CHUNK
    height = chunks * few_levels
    field = grid_field.reshape(2, band_rows, few_levels, chunks, CHUNK).transpose(0, 1, 3, 2, 4)
    field = field.reshape(2, band_rows, height, CHUNK)
    own_spec = pl.BlockSpec((1, slots), lambda g, *_: (0, 0))
    regroup_scratch = [
        pltpu.VMEM((slots // 128, 8, 128, 128), jnp.float32),
        pltpu.VMEM((slots // 128, 8, 128, 128), jnp.float32),
    ]

    far = pl.BlockSpec(memory_space=pltpu.HBM)
    made_shape = (16 * levels, 4 * levels)

    def matrix_spec(shape):
        return pl.BlockSpec(shape, lambda g, *_: (0, 0))

    def blocks_spec(height):
        return pl.BlockSpec((slots // 2, height, 128), lambda g, *_: (0, 0, 0))

    sums, phasors = pl.pallas_call(
        functools.partial(analysis_kernel, order),
        grid_spec=pltpu.PrefetchScalarGridSpec(
            num_scalar_prefetch=3,
            grid=(1,),
            in_specs=[
                own_spec,
                pl.BlockSpec((spectral_variance.shape[0], 128), lambda g, p, w, wave: (0, wave[0] // 2)),
                far,
            ],
            out_specs=[blocks_spec(24), far],
            scratch_shapes=[
                pltpu.VMEM(field.shape, jnp.bfloat16),
                pltpu.VMEM((17, band_rows, slots), jnp.float32),
                pltpu.VMEM((ROWS, 2 * CHUNK, 2 * slots), jnp.bfloat16),
                pltpu.VMEM((2, ROWS, 8, slots), jnp.float32),
            ] + regroup_scratch + [
                pltpu.SemaphoreType.DMA((band_rows // ROWS,)),
                pltpu.SemaphoreType.DMA((band_rows // ROWS,)),
            ],
        ),
        out_shape=[
            jax.ShapeDtypeStruct((slots // 2, 24, 128), jnp.bfloat16),
            jax.ShapeDtypeStruct((15, band_rows, slots), jnp.float32),
        ],
        compiler_params=params,
        name="analysis",
    )(points, weights, wave.reshape(1), own, spectral_variance, field)

    arrived = exchange(sums)

    phasors_spec = pl.BlockSpec((15, band_rows, slots), lambda g, *_: (0, 0, 0))
    table_shape = (band_rows // 2 - BUILT * (ROWS // 2), 2 * slots, 2 * CHUNK)
    table, made = pl.pallas_call(
        table_kernel,
        grid=(1,),
        in_specs=[phasors_spec, matrix_spec((levels, levels))],
        out_specs=[far, matrix_spec(made_shape)],
        scratch_shapes=[
            pltpu.VMEM(table_shape, jnp.bfloat16),
            pltpu.VMEM((ROWS, CHUNK, 2 * slots), jnp.bfloat16),
            pltpu.SemaphoreType.DMA((band_rows // ROWS - BUILT,)),
        ],
        out_shape=[
            jax.ShapeDtypeStruct(table_shape, jnp.bfloat16),
            jax.ShapeDtypeStruct(made_shape, jnp.bfloat16),
        ],
        compiler_params=pltpu.CompilerParams(vmem_limit_bytes=50 * 1024 * 1024),
        cost_estimate=pl.CostEstimate(flops=8 * 10**9, bytes_accessed=9 * 10**6, transcendentals=0),
        name="tables",
    )(phasors, vertical)

    remixed = pl.pallas_call(
        functools.partial(spectral_kernel, order),
        grid_spec=pltpu.PrefetchScalarGridSpec(
            num_scalar_prefetch=1,
            grid=(1,),
            in_specs=[blocks_spec(24), far, matrix_spec(made_shape)],
            out_specs=blocks_spec(16),
            scratch_shapes=[
                pltpu.VMEM((4, 2 * levels, rows), jnp.bfloat16),
                pltpu.VMEM((4, 2 * levels, rows), jnp.float32),
                pltpu.VMEM((2, 2, half_degree, rows), jnp.bfloat16),
                pltpu.SemaphoreType.DMA((2, 2)),
            ],
        ),
        out_shape=jax.ShapeDtypeStruct((slots // 2, 16, 128), jnp.bfloat16),
        compiler_params=pltpu.CompilerParams(vmem_limit_bytes=50 * 1024 * 1024),
        name="spectral",
    )(place, arrived, legendre, made)

    returned = exchange(remixed)

    smoothed = pl.pallas_call(
        functools.partial(synthesis_kernel, order),
        grid_spec=pltpu.PrefetchScalarGridSpec(
            num_scalar_prefetch=1,
            grid=(1,),
            in_specs=[own_spec, blocks_spec(16), far, phasors_spec],
            out_specs=far,
            scratch_shapes=[
                pltpu.VMEM(field.shape, jnp.bfloat16),
                pltpu.VMEM(table_shape, jnp.bfloat16),
                pltpu.VMEM((ROWS, CHUNK, 2 * slots), jnp.bfloat16),
                pltpu.VMEM((slots // 128, 8, 128, 128), jnp.float32),
                pltpu.VMEM((slots // 128, 128, 8, 128), jnp.float32),
                pltpu.SemaphoreType.DMA((band_rows // ROWS - BUILT,)),
                pltpu.SemaphoreType.DMA((band_rows // ROWS,)),
            ],
        ),
        out_shape=jax.ShapeDtypeStruct(field.shape, jnp.bfloat16),
        compiler_params=pltpu.CompilerParams(vmem_limit_bytes=50 * 1024 * 1024),
        name="synthesis",
    )(points, own, returned, table, phasors)
    smoothed = smoothed.reshape(2, band_rows, chunks, few_levels, CHUNK).transpose(0, 1, 3, 2, 4)
    return smoothed.reshape(grid_field.shape)


def solution(mesh):
    return jax.shard_map(
        local,
        mesh=mesh,
        in_specs=(
            P(None, "lat", "wave", None),
            P("lat"),
            P("lat"),
            P(),
            P("wave", None, None, None),
            P("lat", None),
            P(),
        ),
        out_specs=P(None, "lat", "wave", None),
        check_vma=False,
    )
```

```python
import functools

import jax
import jax.numpy as jnp
import numpy as np
from jax import lax
from jax.experimental import pallas as pl
from jax.experimental.pallas import tpu as pltpu
from jax.sharding import PartitionSpec as P

ROWS = 8
CHUNK = 128
BUILT = 2
VMEM_LIMIT = 56 * 1024 * 1024

SIN_TERMS = (3.141592640130707, -5.167710083507862, 2.550077523214134, -0.5982912856178576, 0.0776576603009221)
COS_TERMS = (0.9999999532476082, -4.93479283061961, 4.058411352862034, -1.3318765680776314, 0.2196896110917421)


def polynomial(terms, square):
    total = jnp.full_like(square, terms[-1])
    for term in terms[-2::-1]:
        total = total * square + term
    return total


def phasor(product, length, inverse):
    turns = jnp.floor(product * inverse + 0.5)
    part = (product - turns * length) * inverse
    square = part * part
    sine = part * polynomial(SIN_TERMS, square)
    cosine = polynomial(COS_TERMS, square)
    return 1.0 - 2.0 * sine * sine, 2.0 * sine * cosine


def multiply(a, b):
    return a[0] * b[0] - a[1] * b[1], a[0] * b[1] + a[1] * b[0]


def square(a):
    return a[0] * a[0] - a[1] * a[1], 2.0 * a[0] * a[1]


def times_transposed(a, b):
    return lax.dot_general(a, b, (((1,), (1,)), ((), ())), preferred_element_type=jnp.float32)


def lengths_by_row(points_ref, first, shape):
    row = lax.broadcasted_iota(jnp.int32, shape, 0)
    lengths = jnp.zeros(shape, jnp.int32)
    for r in range(ROWS):
        lengths = jnp.where(row == r, points_ref[first + r], lengths)
    lengths = lengths.astype(jnp.float32)
    return lengths, 1.0 / lengths


def place_phasors(step_ref, waves, lengths, inverse):
    cosine, sine = phasor(waves, lengths, inverse)
    turn, at = (cosine, -sine), 1
    keep = {1: 0, 2: 2, 4: 4, 8: 6, CHUNK: 10, 2 * CHUNK: 12}
    while True:
        if at in keep:
            step_ref[keep[at]], step_ref[keep[at] + 1] = turn
        if at in (8, 16, 2 * CHUNK):
            step_ref[{8: 8, 16: 9, 2 * CHUNK: 14}[at]] = 2.0 * turn[0]
        if at == 2 * CHUNK:
            break
        turn, at = square(turn), 2 * at


def swap_sublanes(values):
    values = list(values)
    sublane = lax.broadcasted_iota(jnp.int32, values[0].shape, 0)
    for d in (4, 2, 1):
        low = sublane & d == 0
        for a in range(8):
            if a & d == 0:
                first, second = values[a], values[a + d]
                values[a] = jnp.where(low, first, pltpu.roll(second, d, 0))
                values[a + d] = jnp.where(low, pltpu.roll(first, 8 - d, 0), second)
    return values


def steps_of(step_ref, which, r):
    slots = step_ref.shape[2]
    return tuple(jnp.broadcast_to(step_ref[n, r:r + 1, :], (8, slots)) for n in which)


def build_table(table_ref, step_ref, r):
    slots = step_ref.shape[2]
    size = table_ref.shape[0]
    sublane = lax.broadcasted_iota(jnp.int32, (8, slots), 0)
    powers = []
    for n in range(3):
        power = steps_of(step_ref, (2 * n, 2 * n + 1), r)
        powers.append(tuple(jnp.where(sublane & (1 << n) == 0, 1.0 - c, power[c]) for c in range(2)))
    real, imaginary, twice, twice_next = steps_of(step_ref, (6, 7, 8, 9), r)
    values = [multiply(multiply(powers[0], powers[1]), powers[2])]
    values.append(multiply(values[0], (real, imaginary)))
    for n in range(2, size // 8):
        if n < 4:
            values.append(tuple(twice * values[n - 1][c] - values[n - 2][c] for c in range(2)))
        else:
            values.append(tuple(twice_next * values[n - 2][c] - values[n - 4][c] for c in range(2)))
        if n % 2:
            for c in range(2):
                both = jnp.concatenate([values[n - 1][c], values[n][c]], axis=0).astype(jnp.bfloat16)
                table_ref[8 * n - 8:8 * n + 8, c * slots:(c + 1) * slots] = both
        elif n == 2:
            for c in range(2):
                both = jnp.concatenate([values[0][c], values[1][c]], axis=0).astype(jnp.bfloat16)
                table_ref[:16, c * slots:(c + 1) * slots] = both


def analysis_kernel(order, points_ref, weights_ref, wave_ref, owners_ref, variance_ref, field_ref, out_ref,
                    phasors_ref, own_ref, step_ref, table_ref, rows_ref, sums_ref, order_ref, sems, phasor_sems):
    slots = owners_ref.shape[1]
    tiles = [slice(t, t + 128) for t in range(0, slots, 128)]
    rows, height = own_ref.shape[1:3]

    def arrival(g):
        at = pl.ds(g * ROWS, ROWS)
        return pltpu.make_async_copy(field_ref.at[:, at], own_ref.at[:, at], sems.at[g])

    def departure(g):
        at = pl.ds(pl.multiple_of(g * ROWS, ROWS), ROWS)
        return pltpu.make_async_copy(step_ref.at[:, at], phasors_ref.at[:, at], phasor_sems.at[g])

    for g in range(rows // ROWS):
        arrival(g).start()
    waves = jnp.broadcast_to(owners_ref[...].astype(jnp.float32), (ROWS, slots))
    sublane = lax.broadcasted_iota(jnp.int32, (8, slots), 0)
    position = lax.broadcasted_iota(jnp.int32, (height, CHUNK), 0) // 4 * CHUNK
    position = position + lax.broadcasted_iota(jnp.int32, (height, CHUNK), 1)

    def group(g, early):
        first = g * ROWS
        lengths, inverse = lengths_by_row(points_ref, first, (ROWS, slots))
        here = step_ref.at[:, pl.ds(pl.multiple_of(first, ROWS), ROWS)]
        place_phasors(here, waves, lengths, inverse)
        departure(g).start()
        if early:
            for r in range(ROWS):
                build_table(table_ref.at[r], here, r)
        arrival(g).wait()
        for r in range(ROWS):
            length = points_ref[first + r]

            if not early:
                build_table(table_ref.at[r], here, r)
            inside = jnp.where(position < length, 1.0, 0.0).astype(jnp.bfloat16)
            points = jnp.concatenate([own_ref[0, first + r] * inside, own_ref[1, first + r] * inside], axis=0)
            parts = jnp.dot(points, table_ref[r], preferred_element_type=jnp.float32)
            chunk, pair, twice = steps_of(here, (10, 11), r), steps_of(here, (12, 13), r), steps_of(here, (14,), r)[0]
            sums = []
            for h in range(2):
                blocks = [
                    tuple(parts[b:b + 8, c * slots:(c + 1) * slots] for c in range(2))
                    for b in range(h * height, (h + 1) * height, 8)
                ]
                later, total = blocks[-1], tuple(blocks[-2][c] + twice * blocks[-1][c] for c in range(2))
                for part in blocks[-3:0:-1]:
                    later, total = total, tuple(part[c] + (twice * total[c] - later[c]) for c in range(2))
                total = multiply(total, pair)
                sums.append(tuple(total[c] + (blocks[0][c] - later[c]) for c in range(2)))
            scale = weights_ref[first + r] / length.astype(jnp.float32)
            scale = jnp.where(2 * owners_ref[...] < length, scale, 0.0)
            firsts, seconds = [], []
            for c in range(2):
                added, taken = sums[0][c] + sums[1][c], sums[0][c] - sums[1][c]
                firsts.append(jnp.where(sublane < 4, added, pltpu.roll(taken, 4, 0)))
                seconds.append(jnp.where(sublane < 4, pltpu.roll(added, 4, 0), taken))
            seconds = multiply(seconds, chunk)
            for c in range(2):
                rows_ref[c, r] = (firsts[c] + seconds[c]) * scale
        for c in range(2):
            for t, lanes in enumerate(tiles):
                for row, part in enumerate(swap_sublanes([rows_ref[c, r, :, lanes] for r in range(ROWS)])):
                    sums_ref[t, row, pl.ds(pl.multiple_of(c * 64 + first, 8), 8), :] = part

    group(0, True)
    lax.fori_loop(1, rows // ROWS, lambda g, _: (group(g, False), 0)[1], 0)

    for row in range(8):
        for t in range(len(tiles)):
            order_ref[t, row] = sums_ref[t, row].T
    variance = variance_ref[...]
    variance = jnp.where(wave_ref[0] % 2 == 1, pltpu.roll(variance, 64, 1), variance)
    upper = variance.astype(jnp.bfloat16).astype(jnp.float32)
    lane = lax.broadcasted_iota(jnp.int32, variance.shape, 1)
    variance = jnp.where(lane < 64, upper, pltpu.roll(variance - upper, 64, 1)).astype(jnp.bfloat16)
    where = {t: n for n, t in enumerate(order)}
    for slot in range(0, slots, 8):
        at = slice(slot % 128, slot % 128 + 8)
        parts = swap_sublanes([order_ref[slot // 128, row, at, :] for row in range(8)])
        for n in range(0, 8, 2):
            to = where[(slot + n) // 2]
            out_ref[to, :16] = jnp.concatenate(parts[n:n + 2], axis=0).astype(jnp.bfloat16)
            out_ref[to, 16:] = variance
    for g in range(rows // ROWS):
        departure(g).wait()


def matrices_of(made_ref):
    size = made_ref.shape[1]
    return made_ref.at[:size], made_ref.at[size:2 * size], made_ref.at[2 * size:]


def place_matrices(vertical_ref, mix_in_ref, mix_out_ref, parting_ref):
    levels = vertical_ref.shape[0]
    vertical = vertical_ref[...].astype(jnp.float32)
    index = lax.broadcasted_iota(jnp.int32, (4 * levels, levels), 0)
    level = lax.broadcasted_iota(jnp.int32, (4 * levels, levels), 1)
    by_block = jnp.where(level == index // 16 * 4 + index % 4, 1.0, 0.0)
    by_slot = jnp.where(level == index % levels, 1.0, 0.0)
    row = lax.broadcasted_iota(jnp.int32, (4 * levels, 4 * levels), 0)
    col = lax.broadcasted_iota(jnp.int32, (4 * levels, 4 * levels), 1)
    by_rows = jnp.dot(by_block, vertical, preferred_element_type=jnp.float32)
    mix_in = times_transposed(by_slot, by_rows)
    mix_in_ref[...] = jnp.where(row // levels == col % 16 // 4, mix_in, 0.0).astype(jnp.bfloat16)
    mix_out = times_transposed(by_rows, by_slot)
    sign = jnp.where((row % 8 // 4 == 1) & (col // levels % 2 == 1), -1.0, 1.0)
    mix_out_ref[...] = jnp.where(row % 16 // 8 == col // (2 * levels), mix_out * sign, 0.0).astype(jnp.bfloat16)
    degree = lax.broadcasted_iota(jnp.int32, parting_ref.shape, 0)
    degree = degree // 128 * 64 + degree % 64
    lane = lax.broadcasted_iota(jnp.int32, parting_ref.shape, 1)
    parting_ref[...] = jnp.where(degree == 2 * (lane % 128) + lane // 128, 1.0, 0.0).astype(jnp.bfloat16)


def table_kernel(step_ref, vertical_ref, out_ref, made_ref, pairs_ref, table_ref, sems):
    groups = step_ref.shape[1] // ROWS - BUILT

    def departure(g):
        at = pl.ds(g * (ROWS // 2), ROWS // 2)
        return pltpu.make_async_copy(pairs_ref.at[at], out_ref.at[at], sems.at[g])

    def group(g, _):
        here = step_ref.at[:, pl.ds(pl.multiple_of((g + BUILT) * ROWS, ROWS), ROWS)]
        for r in range(ROWS):
            build_table(table_ref.at[r], here, r)
            pairs_ref[g * (ROWS // 2) + r // 2, :, (r % 2) * CHUNK:(r % 2 + 1) * CHUNK] = table_ref[r].T
        departure(g).start()
        return 0

    lax.fori_loop(0, groups, group, 0)
    place_matrices(vertical_ref, *matrices_of(made_ref))
    for g in range(groups):
        departure(g).wait()


def synthesis_kernel(order, points_ref, owners_ref, near_values_ref, far_table_ref, near_turns_ref, out_ref,
                     values_ref, turns_ref, own_ref, table_ref, built_ref, order_ref, coefs_ref,
                     near_sems, table_sems, sems):
    slots = owners_ref.shape[1]
    tiles = [slice(t, t + 128) for t in range(0, slots, 128)]
    rows, height = own_ref.shape[1:3]

    def arrival(g):
        at = pl.ds(g * (ROWS // 2), ROWS // 2)
        return pltpu.make_async_copy(far_table_ref.at[at], table_ref.at[at], table_sems.at[g])

    def departure(g):
        at = pl.ds(g * ROWS, ROWS)
        return pltpu.make_async_copy(own_ref.at[:, at], out_ref.at[:, at], sems.at[g])

    near = [
        pltpu.make_async_copy(near_values_ref, values_ref, near_sems.at[0]),
        pltpu.make_async_copy(near_turns_ref, turns_ref, near_sems.at[1]),
    ]
    for copy in near:
        copy.start()
    for g in range(rows // ROWS - BUILT):
        arrival(g).start()
    near[0].wait()
    where = {t: n for n, t in enumerate(order)}
    for slot in range(0, slots, 8):
        parts = []
        for n in range(0, 8, 2):
            pair = values_ref[where[(slot + n) // 2]].astype(jnp.float32)
            parts += [pair[:8], pair[8:]]
        for row, part in enumerate(swap_sublanes(parts)):
            order_ref[slot // 128, row, slot % 128:slot % 128 + 8, :] = part
    for t in range(len(tiles)):
        for row in range(8):
            order_ref[t, row] = order_ref[t, row].T
        for n in range(0, 128, 8):
            parts = swap_sublanes([order_ref[t, row, n:n + 8, :] for row in range(8)])
            for at, part in enumerate(parts):
                coefs_ref[t, n + at] = part

    doubling = jnp.where(owners_ref[...] == 0, 1.0, 2.0)
    sublane = lax.broadcasted_iota(jnp.int32, (8, slots), 0)
    position = lax.broadcasted_iota(jnp.int32, (height, CHUNK), 0) // 4 * CHUNK
    position = position + lax.broadcasted_iota(jnp.int32, (height, CHUNK), 1)

    def group(g, built):
        first = g * ROWS
        if built:
            here = turns_ref.at[:, pl.ds(pl.multiple_of(first, ROWS), ROWS)]
        else:
            arrival(g - BUILT).wait()
        for r in range(ROWS):
            row = first + r
            length = points_ref[row]
            turns = [jnp.broadcast_to(turns_ref[n, pl.ds(row, 1), :], (8, slots)) for n in range(10, 15)]
            chunk, pair, twice = (turns[0], -turns[1]), (turns[2], -turns[3]), turns[4]
            scale = jnp.where(2 * owners_ref[...] < length, doubling, 0.0)
            start = tuple(jnp.where(sublane < 4, 1.0 - c, chunk[c]) * scale for c in range(2))
            values = [
                [coefs_ref[t, c * 64 + row] for t in range(len(tiles))]
                for c in range(2)
            ]
            values = [jnp.concatenate(part, axis=1) for part in values]
            others = [pltpu.roll(part, 4, 0) for part in values]
            turned = []
            for low, high in ((values, others), (others, values)):
                before = multiply(start, [jnp.where(sublane < 4, low[c], high[c]) for c in range(2)])
                value = multiply(before, pair)
                turned += [jnp.concatenate(before, axis=1), jnp.concatenate(value, axis=1)]
                for _ in range(2, height // 8):
                    before, value = value, tuple(twice * value[c] - before[c] for c in range(2))
                    turned.append(jnp.concatenate(value, axis=1))
            turned = jnp.concatenate(turned, axis=0).astype(jnp.bfloat16)
            if built:
                build_table(built_ref.at[r], here, r)
                gridded = times_transposed(turned, built_ref[r])
            else:
                table = table_ref[(g - BUILT) * (ROWS // 2) + r // 2, :, (r % 2) * CHUNK:(r % 2 + 1) * CHUNK]
                gridded = jnp.dot(turned, table, preferred_element_type=jnp.float32)
            for h in range(2):
                own_ref[h, row] = jnp.where(
                    position < length, gridded[h * height:(h + 1) * height], 0.0
                ).astype(jnp.bfloat16)
        departure(g).start()

    near[1].wait()
    for start, end, built in ((0, BUILT, True), (BUILT, rows // ROWS, False)):
        lax.fori_loop(start, end, lambda g, _, built=built: (group(g, built), 0)[1], 0)
    for g in range(rows // ROWS):
        departure(g).wait()


def swap_halves(first, second):
    low = lax.broadcasted_iota(jnp.int32, first.shape, 1) < 64
    return (
        jnp.where(low, first, pltpu.roll(second, 64, 1)),
        jnp.where(low, pltpu.roll(first, 64, 1), second),
    )


def spectral_kernel(order, place_ref, near_values_ref, legendre_ref, near_made_ref, out_ref,
                    values_ref, made_ref, mixed_ref, back_ref, own_ref, near_sems, sems):
    levels = made_ref.shape[1] // 4
    near = [
        pltpu.make_async_copy(near_made_ref, made_ref, near_sems.at[0]),
        pltpu.make_async_copy(near_values_ref, values_ref, near_sems.at[1]),
    ]
    copies = {}
    for slot in range(2):
        for q in range(2):
            copies[slot, q] = pltpu.make_async_copy(
                legendre_ref.at[place_ref[0] + slot, q], own_ref.at[slot, q], sems.at[slot, q]
            )
            copies[slot, q].start()
    for copy in near:
        copy.start()
    for copy in near:
        copy.wait()
    mix_in, mix_out, parting = (part[...] for part in matrices_of(made_ref))
    where = {t: n for n, t in enumerate(order)}
    for p in range(4):
        bands = [
            jnp.concatenate([values_ref[where[w * 8 + v], :16] for w in range(16)], axis=0)
            for v in (2 * p, 2 * p + 1)
        ]
        mixed = jnp.dot(mix_in, jnp.concatenate(bands, axis=1), preferred_element_type=jnp.float32)
        for c, part in enumerate(swap_halves(mixed[:, :128], mixed[:, 128:])):
            part = part.astype(jnp.bfloat16)
            for k in range(4):
                mixed_ref[k, c * levels:(c + 1) * levels, p * 128:(p + 1) * 128] = (
                    part[k * levels:(k + 1) * levels]
                )
    halves = [
        jnp.concatenate([values_ref[where[w * 8 + v], 16:].astype(jnp.float32) for v in range(8)], axis=0)
        for w in range(16)
    ]
    halves = jnp.concatenate([jnp.concatenate(halves[n:n + 4], axis=1) for n in range(0, 16, 4)], axis=0)
    parted = jnp.dot(halves.astype(jnp.bfloat16), parting, preferred_element_type=jnp.float32)
    parted = [parted[n * levels:(n + 1) * levels] for n in range(4)]
    spreads = [jnp.concatenate([part[:, q * 128:(q + 1) * 128] for part in parted], axis=1) for q in range(2)]
    for slot in range(2):
        parity = place_ref[1 + slot]
        for q in range(2):
            s = (q + parity) % 2
            copies[slot, q].wait()
            values = own_ref[slot, q]
            coefficient = times_transposed(mixed_ref[2 * slot + s], values)
            spread = spreads[q]
            scaled = coefficient * jnp.concatenate([spread, spread], axis=0)
            back_ref[2 * slot + s] = jnp.dot(
                scaled.astype(jnp.bfloat16), values, preferred_element_type=jnp.float32
            )
    for p in range(4):
        lanes = slice(p * 128, (p + 1) * 128)
        halves = [
            jnp.concatenate([back_ref[k, c * levels:(c + 1) * levels, lanes] for k in range(4)], axis=0)
            for c in range(2)
        ]
        parts = jnp.concatenate(swap_halves(*halves), axis=1).astype(jnp.bfloat16)
        remixed = jnp.dot(mix_out, parts, preferred_element_type=jnp.float32).astype(jnp.bfloat16)
        for n in range(2):
            for w in range(16):
                out_ref[where[w * 8 + 2 * p + n]] = remixed[16 * w:16 * w + 16, n * 128:(n + 1) * 128]


def local(grid_field, points, weights, owners, legendre, spectral_variance, vertical):
    _, band_rows, few_levels, longitudes = grid_field.shape
    slots = owners.shape[0]
    levels = vertical.shape[0]
    half_degree, rows = legendre.shape[2:]
    wave, lat = lax.axis_index("wave"), lax.axis_index("lat")
    own = owners.reshape(1, slots)
    parities = lax.dynamic_slice_in_dim(owners, 2 * (wave * lax.axis_size("lat") + lat), 2, 0) % 2
    place = jnp.concatenate([(2 * lat).reshape(1), parities])
    params = pltpu.CompilerParams(vmem_limit_bytes=VMEM_LIMIT)

    order = [int(t) for t in np.random.RandomState(5).permutation(slots // 2)]
    exchange = functools.partial(
        lax.all_to_all, axis_name=("wave", "lat"), split_axis=0, concat_axis=0, axis_index_groups=[order], tiled=True
    )

    chunks = longitudes // CHUNK
    height = chunks * few_levels
    field = grid_field.reshape(2, band_rows, few_levels, chunks, CHUNK).transpose(0, 1, 3, 2, 4)
    field = field.reshape(2, band_rows, height, CHUNK)
    own_spec = pl.BlockSpec((1, slots), lambda g, *_: (0, 0))
    regroup_scratch = [
        pltpu.VMEM((slots // 128, 8, 128, 128), jnp.float32),
        pltpu.VMEM((slots // 128, 8, 128, 128), jnp.float32),
    ]

    far = pl.BlockSpec(memory_space=pltpu.HBM)
    anywhere = pl.BlockSpec(memory_space=pl.ANY)
    made_shape = (16 * levels, 4 * levels)

    def matrix_spec(shape):
        return pl.BlockSpec(shape, lambda g, *_: (0, 0))

    def blocks_spec(height):
        return pl.BlockSpec((slots // 2, height, 128), lambda g, *_: (0, 0, 0))

    sums, phasors = pl.pallas_call(
        functools.partial(analysis_kernel, order),
        grid_spec=pltpu.PrefetchScalarGridSpec(
            num_scalar_prefetch=3,
            grid=(1,),
            in_specs=[
                own_spec,
                pl.BlockSpec((spectral_variance.shape[0], 128), lambda g, p, w, wave: (0, wave[0] // 2)),
                far,
            ],
            out_specs=[blocks_spec(24), far],
            scratch_shapes=[
                pltpu.VMEM(field.shape, jnp.bfloat16),
                pltpu.VMEM((15, band_rows, slots), jnp.float32),
                pltpu.VMEM((ROWS, CHUNK, 2 * slots), jnp.bfloat16),
                pltpu.VMEM((2, ROWS, 8, slots), jnp.float32),
            ] + regroup_scratch + [
                pltpu.SemaphoreType.DMA((band_rows // ROWS,)),
                pltpu.SemaphoreType.DMA((band_rows // ROWS,)),
            ],
        ),
        out_shape=[
            jax.ShapeDtypeStruct((slots // 2, 24, 128), jnp.bfloat16),
            jax.ShapeDtypeStruct((15, band_rows, slots), jnp.float32),
        ],
        compiler_params=params,
        name="analysis",
    )(points, weights, wave.reshape(1), own, spectral_variance, field)

    arrived = exchange(sums)

    phasors_spec = pl.BlockSpec((15, band_rows, slots), lambda g, *_: (0, 0, 0))
    table_shape = (band_rows // 2 - BUILT * (ROWS // 2), 2 * slots, 2 * CHUNK)
    table, made = pl.pallas_call(
        table_kernel,
        grid=(1,),
        in_specs=[phasors_spec, matrix_spec((levels, levels))],
        out_specs=[far, matrix_spec(made_shape)],
        scratch_shapes=[
            pltpu.VMEM(table_shape, jnp.bfloat16),
            pltpu.VMEM((ROWS, CHUNK, 2 * slots), jnp.bfloat16),
            pltpu.SemaphoreType.DMA((band_rows // ROWS - BUILT,)),
        ],
        out_shape=[
            jax.ShapeDtypeStruct(table_shape, jnp.bfloat16),
            jax.ShapeDtypeStruct(made_shape, jnp.bfloat16),
        ],
        compiler_params=pltpu.CompilerParams(vmem_limit_bytes=50 * 1024 * 1024),
        cost_estimate=pl.CostEstimate(flops=8 * 10**9, bytes_accessed=9 * 10**6, transcendentals=0),
        name="tables",
    )(phasors, vertical)

    remixed = pl.pallas_call(
        functools.partial(spectral_kernel, order),
        grid_spec=pltpu.PrefetchScalarGridSpec(
            num_scalar_prefetch=1,
            grid=(1,),
            in_specs=[anywhere, far, anywhere],
            out_specs=blocks_spec(16),
            scratch_shapes=[
                pltpu.VMEM((slots // 2, 24, 128), jnp.bfloat16),
                pltpu.VMEM(made_shape, jnp.bfloat16),
                pltpu.VMEM((4, 2 * levels, rows), jnp.bfloat16),
                pltpu.VMEM((4, 2 * levels, rows), jnp.float32),
                pltpu.VMEM((2, 2, half_degree, rows), jnp.bfloat16),
                pltpu.SemaphoreType.DMA((2,)),
                pltpu.SemaphoreType.DMA((2, 2)),
            ],
        ),
        out_shape=jax.ShapeDtypeStruct((slots // 2, 16, 128), jnp.bfloat16),
        compiler_params=pltpu.CompilerParams(vmem_limit_bytes=50 * 1024 * 1024),
        name="spectral",
    )(place, arrived, legendre, made)

    returned = exchange(remixed)

    smoothed = pl.pallas_call(
        functools.partial(synthesis_kernel, order),
        grid_spec=pltpu.PrefetchScalarGridSpec(
            num_scalar_prefetch=1,
            grid=(1,),
            in_specs=[own_spec, anywhere, far, anywhere],
            out_specs=far,
            scratch_shapes=[
                pltpu.VMEM((slots // 2, 16, 128), jnp.bfloat16),
                pltpu.VMEM((15, band_rows, slots), jnp.float32),
                pltpu.VMEM(field.shape, jnp.bfloat16),
                pltpu.VMEM(table_shape, jnp.bfloat16),
                pltpu.VMEM((ROWS, CHUNK, 2 * slots), jnp.bfloat16),
                pltpu.VMEM((slots // 128, 8, 128, 128), jnp.float32),
                pltpu.VMEM((slots // 128, 128, 8, 128), jnp.float32),
                pltpu.SemaphoreType.DMA((2,)),
                pltpu.SemaphoreType.DMA((band_rows // ROWS - BUILT,)),
                pltpu.SemaphoreType.DMA((band_rows // ROWS,)),
            ],
        ),
        out_shape=jax.ShapeDtypeStruct(field.shape, jnp.bfloat16),
        compiler_params=pltpu.CompilerParams(vmem_limit_bytes=50 * 1024 * 1024),
        name="synthesis",
    )(points, own, returned, table, phasors)
    smoothed = smoothed.reshape(2, band_rows, chunks, few_levels, CHUNK).transpose(0, 1, 3, 2, 4)
    return smoothed.reshape(grid_field.shape)


def solution(mesh):
    return jax.shard_map(
        local,
        mesh=mesh,
        in_specs=(
            P(None, "lat", "wave", None),
            P("lat"),
            P("lat"),
            P(),
            P("wave", None, None, None),
            P("lat", None),
            P(),
        ),
        out_specs=P(None, "lat", "wave", None),
        check_vma=False,
    )
```

```python
import functools

import jax
import jax.numpy as jnp
import numpy as np
from jax import lax
from jax.experimental import pallas as pl
from jax.experimental.pallas import tpu as pltpu
from jax.sharding import PartitionSpec as P

ROWS = 8
CHUNK = 128
BUILT = 2
VMEM_LIMIT = 56 * 1024 * 1024

SIN_TERMS = (3.141592640130707, -5.167710083507862, 2.550077523214134, -0.5982912856178576, 0.0776576603009221)
COS_TERMS = (0.9999999532476082, -4.93479283061961, 4.058411352862034, -1.3318765680776314, 0.2196896110917421)


def polynomial(terms, square):
    total = jnp.full_like(square, terms[-1])
    for term in terms[-2::-1]:
        total = total * square + term
    return total


def phasor(product, length, inverse):
    turns = jnp.floor(product * inverse + 0.5)
    part = (product - turns * length) * inverse
    square = part * part
    sine = part * polynomial(SIN_TERMS, square)
    cosine = polynomial(COS_TERMS, square)
    return 1.0 - 2.0 * sine * sine, 2.0 * sine * cosine


def multiply(a, b):
    return a[0] * b[0] - a[1] * b[1], a[0] * b[1] + a[1] * b[0]


def square(a):
    return a[0] * a[0] - a[1] * a[1], 2.0 * a[0] * a[1]


def times_transposed(a, b):
    return lax.dot_general(a, b, (((1,), (1,)), ((), ())), preferred_element_type=jnp.float32)


def lengths_by_row(points_ref, first, shape):
    row = lax.broadcasted_iota(jnp.int32, shape, 0)
    lengths = jnp.zeros(shape, jnp.int32)
    for r in range(ROWS):
        lengths = jnp.where(row == r, points_ref[first + r], lengths)
    lengths = lengths.astype(jnp.float32)
    return lengths, 1.0 / lengths


def place_phasors(step_ref, waves, lengths, inverse):
    cosine, sine = phasor(waves, lengths, inverse)
    turn, at = (cosine, -sine), 1
    keep = {1: 0, 2: 2, 4: 4, 8: 6, CHUNK: 10, 2 * CHUNK: 12}
    while True:
        if at in keep:
            step_ref[keep[at]], step_ref[keep[at] + 1] = turn
        if at in (8, 16, 2 * CHUNK):
            step_ref[{8: 8, 16: 9, 2 * CHUNK: 14}[at]] = 2.0 * turn[0]
        if at == 2 * CHUNK:
            break
        turn, at = square(turn), 2 * at


def swap_sublanes(values):
    values = list(values)
    sublane = lax.broadcasted_iota(jnp.int32, values[0].shape, 0)
    for d in (4, 2, 1):
        low = sublane & d == 0
        for a in range(8):
            if a & d == 0:
                first, second = values[a], values[a + d]
                values[a] = jnp.where(low, first, pltpu.roll(second, d, 0))
                values[a + d] = jnp.where(low, pltpu.roll(first, 8 - d, 0), second)
    return values


def steps_of(step_ref, which, r):
    slots = step_ref.shape[2]
    return tuple(jnp.broadcast_to(step_ref[n, r:r + 1, :], (8, slots)) for n in which)


def build_table(table_ref, step_ref, r):
    slots = step_ref.shape[2]
    size = table_ref.shape[0]
    sublane = lax.broadcasted_iota(jnp.int32, (8, slots), 0)
    powers = []
    for n in range(3):
        power = steps_of(step_ref, (2 * n, 2 * n + 1), r)
        powers.append(tuple(jnp.where(sublane & (1 << n) == 0, 1.0 - c, power[c]) for c in range(2)))
    real, imaginary, twice, twice_next = steps_of(step_ref, (6, 7, 8, 9), r)
    values = [multiply(multiply(powers[0], powers[1]), powers[2])]
    values.append(multiply(values[0], (real, imaginary)))
    for n in range(2, size // 8):
        if n < 4:
            values.append(tuple(twice * values[n - 1][c] - values[n - 2][c] for c in range(2)))
        else:
            values.append(tuple(twice_next * values[n - 2][c] - values[n - 4][c] for c in range(2)))
        if n % 2:
            for c in range(2):
                both = jnp.concatenate([values[n - 1][c], values[n][c]], axis=0).astype(jnp.bfloat16)
                table_ref[8 * n - 8:8 * n + 8, c * slots:(c + 1) * slots] = both
        elif n == 2:
            for c in range(2):
                both = jnp.concatenate([values[0][c], values[1][c]], axis=0).astype(jnp.bfloat16)
                table_ref[:16, c * slots:(c + 1) * slots] = both


def analysis_kernel(order, points_ref, weights_ref, wave_ref, owners_ref, variance_ref, field_ref, out_ref,
                    phasors_ref, own_ref, step_ref, table_ref, rows_ref, sums_ref, order_ref, sems, phasor_sems):
    slots = owners_ref.shape[1]
    tiles = [slice(t, t + 128) for t in range(0, slots, 128)]
    rows, height = own_ref.shape[1:3]

    def arrival(g):
        at = pl.ds(g * ROWS, ROWS)
        return pltpu.make_async_copy(field_ref.at[:, at], own_ref.at[:, at], sems.at[g])

    def departure(g):
        at = pl.ds(pl.multiple_of(g * ROWS, ROWS), ROWS)
        return pltpu.make_async_copy(step_ref.at[:, at], phasors_ref.at[:, at], phasor_sems.at[g])

    for g in range(rows // ROWS):
        arrival(g).start()
    waves = jnp.broadcast_to(owners_ref[...].astype(jnp.float32), (ROWS, slots))
    sublane = lax.broadcasted_iota(jnp.int32, (8, slots), 0)
    position = lax.broadcasted_iota(jnp.int32, (height, CHUNK), 0) // 4 * CHUNK
    position = position + lax.broadcasted_iota(jnp.int32, (height, CHUNK), 1)

    def group(g, _):
        first = g * ROWS
        lengths, inverse = lengths_by_row(points_ref, first, (ROWS, slots))
        here = step_ref.at[:, pl.ds(pl.multiple_of(first, ROWS), ROWS)]
        place_phasors(here, waves, lengths, inverse)
        departure(g).start()
        arrival(g).wait()
        for r in range(ROWS):
            length = points_ref[first + r]

            build_table(table_ref.at[r], here, r)
            inside = jnp.where(position < length, 1.0, 0.0).astype(jnp.bfloat16)
            points = jnp.concatenate([own_ref[0, first + r] * inside, own_ref[1, first + r] * inside], axis=0)
            parts = jnp.dot(points, table_ref[r], preferred_element_type=jnp.float32)
            chunk, pair, twice = steps_of(here, (10, 11), r), steps_of(here, (12, 13), r), steps_of(here, (14,), r)[0]
            sums = []
            for h in range(2):
                blocks = [
                    tuple(parts[b:b + 8, c * slots:(c + 1) * slots] for c in range(2))
                    for b in range(h * height, (h + 1) * height, 8)
                ]
                later, total = blocks[-1], tuple(blocks[-2][c] + twice * blocks[-1][c] for c in range(2))
                for part in blocks[-3:0:-1]:
                    later, total = total, tuple(part[c] + (twice * total[c] - later[c]) for c in range(2))
                total = multiply(total, pair)
                sums.append(tuple(total[c] + (blocks[0][c] - later[c]) for c in range(2)))
            scale = weights_ref[first + r] / length.astype(jnp.float32)
            scale = jnp.where(2 * owners_ref[...] < length, scale, 0.0)
            firsts, seconds = [], []
            for c in range(2):
                added, taken = sums[0][c] + sums[1][c], sums[0][c] - sums[1][c]
                firsts.append(jnp.where(sublane < 4, added, pltpu.roll(taken, 4, 0)))
                seconds.append(jnp.where(sublane < 4, pltpu.roll(added, 4, 0), taken))
            seconds = multiply(seconds, chunk)
            for c in range(2):
                rows_ref[c, r] = (firsts[c] + seconds[c]) * scale
        for c in range(2):
            for t, lanes in enumerate(tiles):
                for row, part in enumerate(swap_sublanes([rows_ref[c, r, :, lanes] for r in range(ROWS)])):
                    sums_ref[t, row, pl.ds(pl.multiple_of(c * 64 + first, 8), 8), :] = part
        return 0

    lax.fori_loop(0, rows // ROWS, group, 0)

    for row in range(8):
        for t in range(len(tiles)):
            order_ref[t, row] = sums_ref[t, row].T
    variance = variance_ref[...]
    variance = jnp.where(wave_ref[0] % 2 == 1, pltpu.roll(variance, 64, 1), variance)
    upper = variance.astype(jnp.bfloat16).astype(jnp.float32)
    lane = lax.broadcasted_iota(jnp.int32, variance.shape, 1)
    variance = jnp.where(lane < 64, upper, pltpu.roll(variance - upper, 64, 1)).astype(jnp.bfloat16)
    where = {t: n for n, t in enumerate(order)}
    for slot in range(0, slots, 8):
        at = slice(slot % 128, slot % 128 + 8)
        parts = swap_sublanes([order_ref[slot // 128, row, at, :] for row in range(8)])
        for n in range(0, 8, 2):
            to = where[(slot + n) // 2]
            out_ref[to, :16] = jnp.concatenate(parts[n:n + 2], axis=0).astype(jnp.bfloat16)
            out_ref[to, 16:] = variance
    for g in range(rows // ROWS):
        departure(g).wait()


def matrices_of(made_ref):
    size = made_ref.shape[1]
    return made_ref.at[:size], made_ref.at[size:2 * size], made_ref.at[2 * size:]


def place_matrices(vertical_ref, mix_in_ref, mix_out_ref, parting_ref):
    levels = vertical_ref.shape[0]
    vertical = vertical_ref[...].astype(jnp.float32)
    index = lax.broadcasted_iota(jnp.int32, (4 * levels, levels), 0)
    level = lax.broadcasted_iota(jnp.int32, (4 * levels, levels), 1)
    by_block = jnp.where(level == index // 16 * 4 + index % 4, 1.0, 0.0)
    by_slot = jnp.where(level == index % levels, 1.0, 0.0)
    row = lax.broadcasted_iota(jnp.int32, (4 * levels, 4 * levels), 0)
    col = lax.broadcasted_iota(jnp.int32, (4 * levels, 4 * levels), 1)
    by_rows = jnp.dot(by_block, vertical, preferred_element_type=jnp.float32)
    mix_in = times_transposed(by_slot, by_rows)
    mix_in_ref[...] = jnp.where(row // levels == col % 16 // 4, mix_in, 0.0).astype(jnp.bfloat16)
    mix_out = times_transposed(by_rows, by_slot)
    sign = jnp.where((row % 8 // 4 == 1) & (col // levels % 2 == 1), -1.0, 1.0)
    mix_out_ref[...] = jnp.where(row % 16 // 8 == col // (2 * levels), mix_out * sign, 0.0).astype(jnp.bfloat16)
    degree = lax.broadcasted_iota(jnp.int32, parting_ref.shape, 0)
    degree = degree // 128 * 64 + degree % 64
    lane = lax.broadcasted_iota(jnp.int32, parting_ref.shape, 1)
    parting_ref[...] = jnp.where(degree == 2 * (lane % 128) + lane // 128, 1.0, 0.0).astype(jnp.bfloat16)


def legendre_copies(legendre_ref, place_ref, own_ref, sems):
    return {
        (slot, q): pltpu.make_async_copy(
            legendre_ref.at[place_ref[0] + slot, q], own_ref.at[slot, q], sems.at[slot, q]
        )
        for slot in range(2) for q in range(2)
    }


def table_kernel(place_ref, step_ref, vertical_ref, legendre_ref, out_ref, made_ref, flipped_ref,
                 pairs_ref, table_ref, own_ref, sems, own_sems):
    copies = legendre_copies(legendre_ref, place_ref, own_ref, own_sems)
    for copy in copies.values():
        copy.start()
    groups = step_ref.shape[1] // ROWS - BUILT

    def departure(g):
        at = pl.ds(g * (ROWS // 2), ROWS // 2)
        return pltpu.make_async_copy(pairs_ref.at[at], out_ref.at[at], sems.at[g])

    def group(g, _):
        here = step_ref.at[:, pl.ds(pl.multiple_of((g + BUILT) * ROWS, ROWS), ROWS)]
        for r in range(ROWS):
            build_table(table_ref.at[r], here, r)
            pairs_ref[g * (ROWS // 2) + r // 2, :, (r % 2) * CHUNK:(r % 2 + 1) * CHUNK] = table_ref[r].T
        departure(g).start()
        return 0

    lax.fori_loop(0, groups, group, 0)
    place_matrices(vertical_ref, *matrices_of(made_ref))
    for (slot, q), copy in copies.items():
        copy.wait()
        flipped_ref[slot, q] = own_ref[slot, q].T
    for g in range(groups):
        departure(g).wait()


def synthesis_kernel(order, points_ref, owners_ref, values_ref, far_table_ref, turns_ref, out_ref,
                     own_ref, table_ref, built_ref, order_ref, coefs_ref, table_sems, sems):
    slots = owners_ref.shape[1]
    tiles = [slice(t, t + 128) for t in range(0, slots, 128)]
    rows, height = own_ref.shape[1:3]

    def arrival(g):
        at = pl.ds(g * (ROWS // 2), ROWS // 2)
        return pltpu.make_async_copy(far_table_ref.at[at], table_ref.at[at], table_sems.at[g])

    def departure(g):
        at = pl.ds(g * ROWS, ROWS)
        return pltpu.make_async_copy(own_ref.at[:, at], out_ref.at[:, at], sems.at[g])

    for g in range(rows // ROWS - BUILT):
        arrival(g).start()
    where = {t: n for n, t in enumerate(order)}
    for slot in range(0, slots, 8):
        parts = []
        for n in range(0, 8, 2):
            pair = values_ref[where[(slot + n) // 2]].astype(jnp.float32)
            parts += [pair[:8], pair[8:]]
        for row, part in enumerate(swap_sublanes(parts)):
            order_ref[slot // 128, row, slot % 128:slot % 128 + 8, :] = part
    for t in range(len(tiles)):
        for row in range(8):
            order_ref[t, row] = order_ref[t, row].T
        for n in range(0, 128, 8):
            parts = swap_sublanes([order_ref[t, row, n:n + 8, :] for row in range(8)])
            for at, part in enumerate(parts):
                coefs_ref[t, n + at] = part

    doubling = jnp.where(owners_ref[...] == 0, 1.0, 2.0)
    sublane = lax.broadcasted_iota(jnp.int32, (8, slots), 0)
    position = lax.broadcasted_iota(jnp.int32, (height, CHUNK), 0) // 4 * CHUNK
    position = position + lax.broadcasted_iota(jnp.int32, (height, CHUNK), 1)

    def group(g, built):
        first = g * ROWS
        if built:
            here = turns_ref.at[:, pl.ds(pl.multiple_of(first, ROWS), ROWS)]
        else:
            arrival(g - BUILT).wait()
        for r in range(ROWS):
            row = first + r
            length = points_ref[row]
            turns = [jnp.broadcast_to(turns_ref[n, pl.ds(row, 1), :], (8, slots)) for n in range(10, 15)]
            chunk, pair, twice = (turns[0], -turns[1]), (turns[2], -turns[3]), turns[4]
            scale = jnp.where(2 * owners_ref[...] < length, doubling, 0.0)
            start = tuple(jnp.where(sublane < 4, 1.0 - c, chunk[c]) * scale for c in range(2))
            values = [
                [coefs_ref[t, c * 64 + row] for t in range(len(tiles))]
                for c in range(2)
            ]
            values = [jnp.concatenate(part, axis=1) for part in values]
            others = [pltpu.roll(part, 4, 0) for part in values]
            turned = []
            for low, high in ((values, others), (others, values)):
                before = multiply(start, [jnp.where(sublane < 4, low[c], high[c]) for c in range(2)])
                value = multiply(before, pair)
                turned += [jnp.concatenate(before, axis=1), jnp.concatenate(value, axis=1)]
                for _ in range(2, height // 8):
                    before, value = value, tuple(twice * value[c] - before[c] for c in range(2))
                    turned.append(jnp.concatenate(value, axis=1))
            turned = jnp.concatenate(turned, axis=0).astype(jnp.bfloat16)
            if built:
                build_table(built_ref.at[r], here, r)
                gridded = times_transposed(turned, built_ref[r])
            else:
                table = table_ref[(g - BUILT) * (ROWS // 2) + r // 2, :, (r % 2) * CHUNK:(r % 2 + 1) * CHUNK]
                gridded = jnp.dot(turned, table, preferred_element_type=jnp.float32)
            for h in range(2):
                own_ref[h, row] = jnp.where(
                    position < length, gridded[h * height:(h + 1) * height], 0.0
                ).astype(jnp.bfloat16)
        departure(g).start()

    for start, end, built in ((0, BUILT, True), (BUILT, rows // ROWS, False)):
        lax.fori_loop(start, end, lambda g, _, built=built: (group(g, built), 0)[1], 0)
    for g in range(rows // ROWS):
        departure(g).wait()


def swap_halves(first, second):
    low = lax.broadcasted_iota(jnp.int32, first.shape, 1) < 64
    return (
        jnp.where(low, first, pltpu.roll(second, 64, 1)),
        jnp.where(low, pltpu.roll(first, 64, 1), second),
    )


def spectral_kernel(order, place_ref, values_ref, legendre_ref, made_ref, near_flipped_ref, out_ref,
                    mixed_ref, back_ref, own_ref, flipped_ref, sems, flipped_sems):
    levels = made_ref.shape[1] // 4
    copies = legendre_copies(legendre_ref, place_ref, own_ref, sems)
    flips = {
        at: pltpu.make_async_copy(near_flipped_ref.at[at], flipped_ref.at[at], flipped_sems.at[at]) for at in copies
    }
    for at in copies:
        flips[at].start()
        copies[at].start()
    mix_in, mix_out, parting = (part[...] for part in matrices_of(made_ref))
    where = {t: n for n, t in enumerate(order)}
    for p in range(4):
        bands = [
            jnp.concatenate([values_ref[where[w * 8 + v], :16] for w in range(16)], axis=0)
            for v in (2 * p, 2 * p + 1)
        ]
        mixed = jnp.dot(mix_in, jnp.concatenate(bands, axis=1), preferred_element_type=jnp.float32)
        for c, part in enumerate(swap_halves(mixed[:, :128], mixed[:, 128:])):
            part = part.astype(jnp.bfloat16)
            for k in range(4):
                mixed_ref[k, c * levels:(c + 1) * levels, p * 128:(p + 1) * 128] = (
                    part[k * levels:(k + 1) * levels]
                )
    halves = [
        jnp.concatenate([values_ref[where[w * 8 + v], 16:].astype(jnp.float32) for v in range(8)], axis=0)
        for w in range(16)
    ]
    halves = jnp.concatenate([jnp.concatenate(halves[n:n + 4], axis=1) for n in range(0, 16, 4)], axis=0)
    parted = jnp.dot(halves.astype(jnp.bfloat16), parting, preferred_element_type=jnp.float32)
    parted = [parted[n * levels:(n + 1) * levels] for n in range(4)]
    spreads = [jnp.concatenate([part[:, q * 128:(q + 1) * 128] for part in parted], axis=1) for q in range(2)]
    for slot in range(2):
        parity = place_ref[1 + slot]
        for q in range(2):
            s = (q + parity) % 2
            flips[slot, q].wait()
            coefficient = jnp.dot(
                mixed_ref[2 * slot + s], flipped_ref[slot, q], preferred_element_type=jnp.float32
            )
            spread = spreads[q]
            scaled = coefficient * jnp.concatenate([spread, spread], axis=0)
            copies[slot, q].wait()
            back_ref[2 * slot + s] = jnp.dot(
                scaled.astype(jnp.bfloat16), own_ref[slot, q], preferred_element_type=jnp.float32
            )
    for p in range(4):
        lanes = slice(p * 128, (p + 1) * 128)
        halves = [
            jnp.concatenate([back_ref[k, c * levels:(c + 1) * levels, lanes] for k in range(4)], axis=0)
            for c in range(2)
        ]
        parts = jnp.concatenate(swap_halves(*halves), axis=1).astype(jnp.bfloat16)
        remixed = jnp.dot(mix_out, parts, preferred_element_type=jnp.float32).astype(jnp.bfloat16)
        for n in range(2):
            for w in range(16):
                out_ref[where[w * 8 + 2 * p + n]] = remixed[16 * w:16 * w + 16, n * 128:(n + 1) * 128]


def local(grid_field, points, weights, owners, legendre, spectral_variance, vertical):
    _, band_rows, few_levels, longitudes = grid_field.shape
    slots = owners.shape[0]
    levels = vertical.shape[0]
    half_degree, rows = legendre.shape[2:]
    wave, lat = lax.axis_index("wave"), lax.axis_index("lat")
    own = owners.reshape(1, slots)
    parities = lax.dynamic_slice_in_dim(owners, 2 * (wave * lax.axis_size("lat") + lat), 2, 0) % 2
    place = jnp.concatenate([(2 * lat).reshape(1), parities])
    params = pltpu.CompilerParams(vmem_limit_bytes=VMEM_LIMIT)

    order = [int(t) for t in np.random.RandomState(5).permutation(slots // 2)]
    exchange = functools.partial(
        lax.all_to_all, axis_name=("wave", "lat"), split_axis=0, concat_axis=0, axis_index_groups=[order], tiled=True
    )

    chunks = longitudes // CHUNK
    height = chunks * few_levels
    field = grid_field.reshape(2, band_rows, few_levels, chunks, CHUNK).transpose(0, 1, 3, 2, 4)
    field = field.reshape(2, band_rows, height, CHUNK)
    own_spec = pl.BlockSpec((1, slots), lambda g, *_: (0, 0))
    regroup_scratch = [
        pltpu.VMEM((slots // 128, 8, 128, 128), jnp.float32),
        pltpu.VMEM((slots // 128, 8, 128, 128), jnp.float32),
    ]

    far = pl.BlockSpec(memory_space=pltpu.HBM)
    made_shape = (16 * levels, 4 * levels)

    def matrix_spec(shape):
        return pl.BlockSpec(shape, lambda g, *_: (0, 0))

    def blocks_spec(height):
        return pl.BlockSpec((slots // 2, height, 128), lambda g, *_: (0, 0, 0))

    sums, phasors = pl.pallas_call(
        functools.partial(analysis_kernel, order),
        grid_spec=pltpu.PrefetchScalarGridSpec(
            num_scalar_prefetch=3,
            grid=(1,),
            in_specs=[
                own_spec,
                pl.BlockSpec((spectral_variance.shape[0], 128), lambda g, p, w, wave: (0, wave[0] // 2)),
                far,
            ],
            out_specs=[blocks_spec(24), far],
            scratch_shapes=[
                pltpu.VMEM(field.shape, jnp.bfloat16),
                pltpu.VMEM((15, band_rows, slots), jnp.float32),
                pltpu.VMEM((ROWS, CHUNK, 2 * slots), jnp.bfloat16),
                pltpu.VMEM((2, ROWS, 8, slots), jnp.float32),
            ] + regroup_scratch + [
                pltpu.SemaphoreType.DMA((band_rows // ROWS,)),
                pltpu.SemaphoreType.DMA((band_rows // ROWS,)),
            ],
        ),
        out_shape=[
            jax.ShapeDtypeStruct((slots // 2, 24, 128), jnp.bfloat16),
            jax.ShapeDtypeStruct((15, band_rows, slots), jnp.float32),
        ],
        compiler_params=params,
        name="analysis",
    )(points, weights, wave.reshape(1), own, spectral_variance, field)

    arrived = exchange(sums)

    phasors_spec = pl.BlockSpec((15, band_rows, slots), lambda g, *_: (0, 0, 0))
    table_shape = (band_rows // 2 - BUILT * (ROWS // 2), 2 * slots, 2 * CHUNK)
    own_shape = (2, 2, half_degree, rows)
    flipped_shape = (2, 2, rows, half_degree)
    table, made, flipped = pl.pallas_call(
        table_kernel,
        grid_spec=pltpu.PrefetchScalarGridSpec(
            num_scalar_prefetch=1,
            grid=(1,),
            in_specs=[phasors_spec, matrix_spec((levels, levels)), far],
            out_specs=[far, matrix_spec(made_shape), pl.BlockSpec(flipped_shape, lambda g, *_: (0, 0, 0, 0))],
            scratch_shapes=[
                pltpu.VMEM(table_shape, jnp.bfloat16),
                pltpu.VMEM((ROWS, CHUNK, 2 * slots), jnp.bfloat16),
                pltpu.VMEM(own_shape, jnp.bfloat16),
                pltpu.SemaphoreType.DMA((band_rows // ROWS - BUILT,)),
                pltpu.SemaphoreType.DMA((2, 2)),
            ],
        ),
        out_shape=[
            jax.ShapeDtypeStruct(table_shape, jnp.bfloat16),
            jax.ShapeDtypeStruct(made_shape, jnp.bfloat16),
            jax.ShapeDtypeStruct(flipped_shape, jnp.bfloat16),
        ],
        compiler_params=pltpu.CompilerParams(vmem_limit_bytes=50 * 1024 * 1024),
        cost_estimate=pl.CostEstimate(flops=8 * 10**9, bytes_accessed=9 * 10**6, transcendentals=0),
        name="tables",
    )(place, phasors, vertical, legendre)

    remixed = pl.pallas_call(
        functools.partial(spectral_kernel, order),
        grid_spec=pltpu.PrefetchScalarGridSpec(
            num_scalar_prefetch=1,
            grid=(1,),
            in_specs=[blocks_spec(24), far, matrix_spec(made_shape), pl.BlockSpec(memory_space=pl.ANY)],
            out_specs=blocks_spec(16),
            scratch_shapes=[
                pltpu.VMEM((4, 2 * levels, rows), jnp.bfloat16),
                pltpu.VMEM((4, 2 * levels, rows), jnp.float32),
                pltpu.VMEM(own_shape, jnp.bfloat16),
                pltpu.VMEM(flipped_shape, jnp.bfloat16),
                pltpu.SemaphoreType.DMA((2, 2)),
                pltpu.SemaphoreType.DMA((2, 2)),
            ],
        ),
        out_shape=jax.ShapeDtypeStruct((slots // 2, 16, 128), jnp.bfloat16),
        compiler_params=pltpu.CompilerParams(vmem_limit_bytes=50 * 1024 * 1024),
        name="spectral",
    )(place, arrived, legendre, made, flipped)

    returned = exchange(remixed)

    smoothed = pl.pallas_call(
        functools.partial(synthesis_kernel, order),
        grid_spec=pltpu.PrefetchScalarGridSpec(
            num_scalar_prefetch=1,
            grid=(1,),
            in_specs=[own_spec, blocks_spec(16), far, phasors_spec],
            out_specs=far,
            scratch_shapes=[
                pltpu.VMEM(field.shape, jnp.bfloat16),
                pltpu.VMEM(table_shape, jnp.bfloat16),
                pltpu.VMEM((ROWS, CHUNK, 2 * slots), jnp.bfloat16),
                pltpu.VMEM((slots // 128, 8, 128, 128), jnp.float32),
                pltpu.VMEM((slots // 128, 128, 8, 128), jnp.float32),
                pltpu.SemaphoreType.DMA((band_rows // ROWS - BUILT,)),
                pltpu.SemaphoreType.DMA((band_rows // ROWS,)),
            ],
        ),
        out_shape=jax.ShapeDtypeStruct(field.shape, jnp.bfloat16),
        compiler_params=pltpu.CompilerParams(vmem_limit_bytes=50 * 1024 * 1024),
        name="synthesis",
    )(points, own, returned, table, phasors)
    smoothed = smoothed.reshape(2, band_rows, chunks, few_levels, CHUNK).transpose(0, 1, 3, 2, 4)
    return smoothed.reshape(grid_field.shape)


def solution(mesh):
    return jax.shard_map(
        local,
        mesh=mesh,
        in_specs=(
            P(None, "lat", "wave", None),
            P("lat"),
            P("lat"),
            P(),
            P("wave", None, None, None),
            P("lat", None),
            P(),
        ),
        out_specs=P(None, "lat", "wave", None),
        check_vma=False,
    )
```

```python
import functools

import jax
import jax.numpy as jnp
import numpy as np
from jax import lax
from jax.experimental import pallas as pl
from jax.experimental.pallas import tpu as pltpu
from jax.sharding import PartitionSpec as P

ROWS = 8
CHUNK = 128
NEAR = 2
VMEM_LIMIT = 56 * 1024 * 1024

SIN_TERMS = (3.141592640130707, -5.167710083507862, 2.550077523214134, -0.5982912856178576, 0.0776576603009221)
COS_TERMS = (0.9999999532476082, -4.93479283061961, 4.058411352862034, -1.3318765680776314, 0.2196896110917421)


def polynomial(terms, square):
    total = jnp.full_like(square, terms[-1])
    for term in terms[-2::-1]:
        total = total * square + term
    return total


def phasor(product, length, inverse):
    turns = jnp.floor(product * inverse + 0.5)
    part = (product - turns * length) * inverse
    square = part * part
    sine = part * polynomial(SIN_TERMS, square)
    cosine = polynomial(COS_TERMS, square)
    return 1.0 - 2.0 * sine * sine, 2.0 * sine * cosine


def multiply(a, b):
    return a[0] * b[0] - a[1] * b[1], a[0] * b[1] + a[1] * b[0]


def square(a):
    return a[0] * a[0] - a[1] * a[1], 2.0 * a[0] * a[1]


def times_transposed(a, b):
    return lax.dot_general(a, b, (((1,), (1,)), ((), ())), preferred_element_type=jnp.float32)


def lengths_by_row(points_ref, first, shape):
    row = lax.broadcasted_iota(jnp.int32, shape, 0)
    lengths = jnp.zeros(shape, jnp.int32)
    for r in range(ROWS):
        lengths = jnp.where(row == r, points_ref[first + r], lengths)
    lengths = lengths.astype(jnp.float32)
    return lengths, 1.0 / lengths


def place_phasors(step_ref, waves, lengths, inverse):
    cosine, sine = phasor(waves, lengths, inverse)
    turn, at = (cosine, -sine), 1
    keep = {1: 0, 2: 2, 4: 4, 8: 6, CHUNK: 10, 2 * CHUNK: 12}
    while True:
        if at in keep:
            step_ref[keep[at]], step_ref[keep[at] + 1] = turn
        if at in (8, 16, 2 * CHUNK):
            step_ref[{8: 8, 16: 9, 2 * CHUNK: 14}[at]] = 2.0 * turn[0]
        if at == 2 * CHUNK:
            break
        turn, at = square(turn), 2 * at


def swap_sublanes(values):
    values = list(values)
    sublane = lax.broadcasted_iota(jnp.int32, values[0].shape, 0)
    for d in (4, 2, 1):
        low = sublane & d == 0
        for a in range(8):
            if a & d == 0:
                first, second = values[a], values[a + d]
                values[a] = jnp.where(low, first, pltpu.roll(second, d, 0))
                values[a + d] = jnp.where(low, pltpu.roll(first, 8 - d, 0), second)
    return values


def steps_of(step_ref, which, r):
    slots = step_ref.shape[2]
    return tuple(jnp.broadcast_to(step_ref[n, r:r + 1, :], (8, slots)) for n in which)


def build_table(table_ref, step_ref, r):
    slots = step_ref.shape[2]
    size = table_ref.shape[0]
    sublane = lax.broadcasted_iota(jnp.int32, (8, slots), 0)
    powers = []
    for n in range(3):
        power = steps_of(step_ref, (2 * n, 2 * n + 1), r)
        powers.append(tuple(jnp.where(sublane & (1 << n) == 0, 1.0 - c, power[c]) for c in range(2)))
    real, imaginary, twice, twice_next = steps_of(step_ref, (6, 7, 8, 9), r)
    values = [multiply(multiply(powers[0], powers[1]), powers[2])]
    values.append(multiply(values[0], (real, imaginary)))
    for n in range(2, size // 8):
        if n < 4:
            values.append(tuple(twice * values[n - 1][c] - values[n - 2][c] for c in range(2)))
        else:
            values.append(tuple(twice_next * values[n - 2][c] - values[n - 4][c] for c in range(2)))
        if n % 2:
            for c in range(2):
                both = jnp.concatenate([values[n - 1][c], values[n][c]], axis=0).astype(jnp.bfloat16)
                table_ref[8 * n - 8:8 * n + 8, c * slots:(c + 1) * slots] = both
        elif n == 2:
            for c in range(2):
                both = jnp.concatenate([values[0][c], values[1][c]], axis=0).astype(jnp.bfloat16)
                table_ref[:16, c * slots:(c + 1) * slots] = both


def analysis_kernel(order, points_ref, weights_ref, wave_ref, owners_ref, variance_ref, field_ref, out_ref,
                    phasors_ref, own_ref, step_ref, table_ref, rows_ref, sums_ref, order_ref, sems, phasor_sems):
    slots = owners_ref.shape[1]
    tiles = [slice(t, t + 128) for t in range(0, slots, 128)]
    rows, height = own_ref.shape[1:3]

    def arrival(g):
        at = pl.ds(g * ROWS, ROWS)
        return pltpu.make_async_copy(field_ref.at[:, at], own_ref.at[:, at], sems.at[g])

    def departure(g):
        at = pl.ds(pl.multiple_of(g * ROWS, ROWS), ROWS)
        return pltpu.make_async_copy(step_ref.at[:, at], phasors_ref.at[:, at], phasor_sems.at[g])

    for g in range(rows // ROWS):
        arrival(g).start()
    waves = jnp.broadcast_to(owners_ref[...].astype(jnp.float32), (ROWS, slots))
    sublane = lax.broadcasted_iota(jnp.int32, (8, slots), 0)
    position = lax.broadcasted_iota(jnp.int32, (height, CHUNK), 0) // 4 * CHUNK
    position = position + lax.broadcasted_iota(jnp.int32, (height, CHUNK), 1)

    def group(g, _):
        first = g * ROWS
        lengths, inverse = lengths_by_row(points_ref, first, (ROWS, slots))
        here = step_ref.at[:, pl.ds(pl.multiple_of(first, ROWS), ROWS)]
        place_phasors(here, waves, lengths, inverse)
        departure(g).start()
        arrival(g).wait()
        for r in range(ROWS):
            length = points_ref[first + r]

            build_table(table_ref.at[r], here, r)
            inside = jnp.where(position < length, 1.0, 0.0).astype(jnp.bfloat16)
            points = jnp.concatenate([own_ref[0, first + r] * inside, own_ref[1, first + r] * inside], axis=0)
            parts = jnp.dot(points, table_ref[r], preferred_element_type=jnp.float32)
            chunk, pair, twice = steps_of(here, (10, 11), r), steps_of(here, (12, 13), r), steps_of(here, (14,), r)[0]
            sums = []
            for h in range(2):
                blocks = [
                    tuple(parts[b:b + 8, c * slots:(c + 1) * slots] for c in range(2))
                    for b in range(h * height, (h + 1) * height, 8)
                ]
                later, total = blocks[-1], tuple(blocks[-2][c] + twice * blocks[-1][c] for c in range(2))
                for part in blocks[-3:0:-1]:
                    later, total = total, tuple(part[c] + (twice * total[c] - later[c]) for c in range(2))
                total = multiply(total, pair)
                sums.append(tuple(total[c] + (blocks[0][c] - later[c]) for c in range(2)))
            scale = weights_ref[first + r] / length.astype(jnp.float32)
            scale = jnp.where(2 * owners_ref[...] < length, scale, 0.0)
            firsts, seconds = [], []
            for c in range(2):
                added, taken = sums[0][c] + sums[1][c], sums[0][c] - sums[1][c]
                firsts.append(jnp.where(sublane < 4, added, pltpu.roll(taken, 4, 0)))
                seconds.append(jnp.where(sublane < 4, pltpu.roll(added, 4, 0), taken))
            seconds = multiply(seconds, chunk)
            for c in range(2):
                rows_ref[c, r] = (firsts[c] + seconds[c]) * scale
        for c in range(2):
            for t, lanes in enumerate(tiles):
                for row, part in enumerate(swap_sublanes([rows_ref[c, r, :, lanes] for r in range(ROWS)])):
                    sums_ref[t, row, pl.ds(pl.multiple_of(c * 64 + first, 8), 8), :] = part
        return 0

    lax.fori_loop(0, rows // ROWS, group, 0)

    for row in range(8):
        for t in range(len(tiles)):
            order_ref[t, row] = sums_ref[t, row].T
    variance = variance_ref[...]
    variance = jnp.where(wave_ref[0] % 2 == 1, pltpu.roll(variance, 64, 1), variance)
    upper = variance.astype(jnp.bfloat16).astype(jnp.float32)
    lane = lax.broadcasted_iota(jnp.int32, variance.shape, 1)
    variance = jnp.where(lane < 64, upper, pltpu.roll(variance - upper, 64, 1)).astype(jnp.bfloat16)
    where = {t: n for n, t in enumerate(order)}
    for slot in range(0, slots, 8):
        at = slice(slot % 128, slot % 128 + 8)
        parts = swap_sublanes([order_ref[slot // 128, row, at, :] for row in range(8)])
        for n in range(0, 8, 2):
            to = where[(slot + n) // 2]
            out_ref[to, :16] = jnp.concatenate(parts[n:n + 2], axis=0).astype(jnp.bfloat16)
            out_ref[to, 16:] = variance
    for g in range(rows // ROWS):
        departure(g).wait()


def matrices_of(made_ref):
    size = made_ref.shape[1]
    return made_ref.at[:size], made_ref.at[size:2 * size], made_ref.at[2 * size:]


def place_matrices(vertical_ref, mix_in_ref, mix_out_ref, parting_ref):
    levels = vertical_ref.shape[0]
    vertical = vertical_ref[...].astype(jnp.float32)
    index = lax.broadcasted_iota(jnp.int32, (4 * levels, levels), 0)
    level = lax.broadcasted_iota(jnp.int32, (4 * levels, levels), 1)
    by_block = jnp.where(level == index // 16 * 4 + index % 4, 1.0, 0.0)
    by_slot = jnp.where(level == index % levels, 1.0, 0.0)
    row = lax.broadcasted_iota(jnp.int32, (4 * levels, 4 * levels), 0)
    col = lax.broadcasted_iota(jnp.int32, (4 * levels, 4 * levels), 1)
    by_rows = jnp.dot(by_block, vertical, preferred_element_type=jnp.float32)
    mix_in = times_transposed(by_slot, by_rows)
    mix_in_ref[...] = jnp.where(row // levels == col % 16 // 4, mix_in, 0.0).astype(jnp.bfloat16)
    mix_out = times_transposed(by_rows, by_slot)
    sign = jnp.where((row % 8 // 4 == 1) & (col // levels % 2 == 1), -1.0, 1.0)
    mix_out_ref[...] = jnp.where(row % 16 // 8 == col // (2 * levels), mix_out * sign, 0.0).astype(jnp.bfloat16)
    degree = lax.broadcasted_iota(jnp.int32, parting_ref.shape, 0)
    degree = degree // 128 * 64 + degree % 64
    lane = lax.broadcasted_iota(jnp.int32, parting_ref.shape, 1)
    parting_ref[...] = jnp.where(degree == 2 * (lane % 128) + lane // 128, 1.0, 0.0).astype(jnp.bfloat16)


def table_kernel(step_ref, vertical_ref, out_ref, near_ref, made_ref, pairs_ref, table_ref, sems):
    groups = step_ref.shape[1] // ROWS - NEAR

    def departure(g):
        at = pl.ds(g * (ROWS // 2), ROWS // 2)
        return pltpu.make_async_copy(pairs_ref.at[at], out_ref.at[at], sems.at[g])

    def group(g, to_ref, at):
        here = step_ref.at[:, pl.ds(pl.multiple_of(g * ROWS, ROWS), ROWS)]
        for r in range(ROWS):
            build_table(table_ref.at[r], here, r)
            to_ref[at * (ROWS // 2) + r // 2, :, (r % 2) * CHUNK:(r % 2 + 1) * CHUNK] = table_ref[r].T

    def far_group(g, _):
        group(g + NEAR, pairs_ref, g)
        departure(g).start()
        return 0

    lax.fori_loop(0, groups, far_group, 0)
    lax.fori_loop(0, NEAR, lambda g, _: (group(g, near_ref, g), 0)[1], 0)
    place_matrices(vertical_ref, *matrices_of(made_ref))
    for g in range(groups):
        departure(g).wait()


def synthesis_kernel(order, points_ref, owners_ref, values_ref, far_table_ref, near_table_ref, turns_ref, out_ref,
                     own_ref, table_ref, order_ref, coefs_ref, table_sems, sems):
    slots = owners_ref.shape[1]
    tiles = [slice(t, t + 128) for t in range(0, slots, 128)]
    rows, height = own_ref.shape[1:3]

    def arrival(g, near):
        to = table_ref.at[pl.ds(g * (ROWS // 2), ROWS // 2)]
        at = pl.ds((g if near else g - NEAR) * (ROWS // 2), ROWS // 2)
        return pltpu.make_async_copy((near_table_ref if near else far_table_ref).at[at], to, table_sems.at[g])

    def departure(g):
        at = pl.ds(g * ROWS, ROWS)
        return pltpu.make_async_copy(own_ref.at[:, at], out_ref.at[:, at], sems.at[g])

    for g in range(rows // ROWS):
        arrival(g, g < NEAR).start()
    where = {t: n for n, t in enumerate(order)}
    for slot in range(0, slots, 8):
        parts = []
        for n in range(0, 8, 2):
            pair = values_ref[where[(slot + n) // 2]].astype(jnp.float32)
            parts += [pair[:8], pair[8:]]
        for row, part in enumerate(swap_sublanes(parts)):
            order_ref[slot // 128, row, slot % 128:slot % 128 + 8, :] = part
    for t in range(len(tiles)):
        for row in range(8):
            order_ref[t, row] = order_ref[t, row].T
        for n in range(0, 128, 8):
            parts = swap_sublanes([order_ref[t, row, n:n + 8, :] for row in range(8)])
            for at, part in enumerate(parts):
                coefs_ref[t, n + at] = part

    doubling = jnp.where(owners_ref[...] == 0, 1.0, 2.0)
    sublane = lax.broadcasted_iota(jnp.int32, (8, slots), 0)
    position = lax.broadcasted_iota(jnp.int32, (height, CHUNK), 0) // 4 * CHUNK
    position = position + lax.broadcasted_iota(jnp.int32, (height, CHUNK), 1)

    def group(g, near):
        first = g * ROWS
        arrival(g, near).wait()
        for r in range(ROWS):
            row = first + r
            length = points_ref[row]
            turns = [jnp.broadcast_to(turns_ref[n, pl.ds(row, 1), :], (8, slots)) for n in range(10, 15)]
            chunk, pair, twice = (turns[0], -turns[1]), (turns[2], -turns[3]), turns[4]
            scale = jnp.where(2 * owners_ref[...] < length, doubling, 0.0)
            start = tuple(jnp.where(sublane < 4, 1.0 - c, chunk[c]) * scale for c in range(2))
            values = [
                [coefs_ref[t, c * 64 + row] for t in range(len(tiles))]
                for c in range(2)
            ]
            values = [jnp.concatenate(part, axis=1) for part in values]
            others = [pltpu.roll(part, 4, 0) for part in values]
            turned = []
            for low, high in ((values, others), (others, values)):
                before = multiply(start, [jnp.where(sublane < 4, low[c], high[c]) for c in range(2)])
                value = multiply(before, pair)
                turned += [jnp.concatenate(before, axis=1), jnp.concatenate(value, axis=1)]
                for _ in range(2, height // 8):
                    before, value = value, tuple(twice * value[c] - before[c] for c in range(2))
                    turned.append(jnp.concatenate(value, axis=1))
            turned = jnp.concatenate(turned, axis=0).astype(jnp.bfloat16)
            table = table_ref[g * (ROWS // 2) + r // 2, :, (r % 2) * CHUNK:(r % 2 + 1) * CHUNK]
            gridded = jnp.dot(turned, table, preferred_element_type=jnp.float32)
            for h in range(2):
                own_ref[h, row] = jnp.where(
                    position < length, gridded[h * height:(h + 1) * height], 0.0
                ).astype(jnp.bfloat16)
        departure(g).start()

    for start, end, near in ((0, NEAR, True), (NEAR, rows // ROWS, False)):
        lax.fori_loop(start, end, lambda g, _, near=near: (group(g, near), 0)[1], 0)
    for g in range(rows // ROWS):
        departure(g).wait()


def swap_halves(first, second):
    low = lax.broadcasted_iota(jnp.int32, first.shape, 1) < 64
    return (
        jnp.where(low, first, pltpu.roll(second, 64, 1)),
        jnp.where(low, pltpu.roll(first, 64, 1), second),
    )


def spectral_kernel(order, place_ref, values_ref, legendre_ref, made_ref, out_ref,
                    mixed_ref, back_ref, own_ref, sems):
    levels = made_ref.shape[1] // 4
    copies = {}
    for slot in range(2):
        for q in range(2):
            copies[slot, q] = pltpu.make_async_copy(
                legendre_ref.at[place_ref[0] + slot, q], own_ref.at[slot, q], sems.at[slot, q]
            )
            copies[slot, q].start()
    mix_in, mix_out, parting = (part[...] for part in matrices_of(made_ref))
    where = {t: n for n, t in enumerate(order)}
    for p in range(4):
        bands = [
            jnp.concatenate([values_ref[where[w * 8 + v], :16] for w in range(16)], axis=0)
            for v in (2 * p, 2 * p + 1)
        ]
        mixed = jnp.dot(mix_in, jnp.concatenate(bands, axis=1), preferred_element_type=jnp.float32)
        for c, part in enumerate(swap_halves(mixed[:, :128], mixed[:, 128:])):
            part = part.astype(jnp.bfloat16)
            for k in range(4):
                mixed_ref[k, c * levels:(c + 1) * levels, p * 128:(p + 1) * 128] = (
                    part[k * levels:(k + 1) * levels]
                )
    halves = [
        jnp.concatenate([values_ref[where[w * 8 + v], 16:].astype(jnp.float32) for v in range(8)], axis=0)
        for w in range(16)
    ]
    halves = jnp.concatenate([jnp.concatenate(halves[n:n + 4], axis=1) for n in range(0, 16, 4)], axis=0)
    parted = jnp.dot(halves.astype(jnp.bfloat16), parting, preferred_element_type=jnp.float32)
    parted = [parted[n * levels:(n + 1) * levels] for n in range(4)]
    spreads = [jnp.concatenate([part[:, q * 128:(q + 1) * 128] for part in parted], axis=1) for q in range(2)]
    for slot in range(2):
        parity = place_ref[1 + slot]
        for q in range(2):
            s = (q + parity) % 2
            copies[slot, q].wait()
            values = own_ref[slot, q]
            coefficient = times_transposed(mixed_ref[2 * slot + s], values)
            spread = spreads[q]
            scaled = coefficient * jnp.concatenate([spread, spread], axis=0)
            back_ref[2 * slot + s] = jnp.dot(
                scaled.astype(jnp.bfloat16), values, preferred_element_type=jnp.float32
            )
    for p in range(4):
        lanes = slice(p * 128, (p + 1) * 128)
        halves = [
            jnp.concatenate([back_ref[k, c * levels:(c + 1) * levels, lanes] for k in range(4)], axis=0)
            for c in range(2)
        ]
        parts = jnp.concatenate(swap_halves(*halves), axis=1).astype(jnp.bfloat16)
        remixed = jnp.dot(mix_out, parts, preferred_element_type=jnp.float32).astype(jnp.bfloat16)
        for n in range(2):
            for w in range(16):
                out_ref[where[w * 8 + 2 * p + n]] = remixed[16 * w:16 * w + 16, n * 128:(n + 1) * 128]


def local(grid_field, points, weights, owners, legendre, spectral_variance, vertical):
    _, band_rows, few_levels, longitudes = grid_field.shape
    slots = owners.shape[0]
    levels = vertical.shape[0]
    half_degree, rows = legendre.shape[2:]
    wave, lat = lax.axis_index("wave"), lax.axis_index("lat")
    own = owners.reshape(1, slots)
    parities = lax.dynamic_slice_in_dim(owners, 2 * (wave * lax.axis_size("lat") + lat), 2, 0) % 2
    place = jnp.concatenate([(2 * lat).reshape(1), parities])
    params = pltpu.CompilerParams(vmem_limit_bytes=VMEM_LIMIT)

    order = [int(t) for t in np.random.RandomState(5).permutation(slots // 2)]
    exchange = functools.partial(
        lax.all_to_all, axis_name=("wave", "lat"), split_axis=0, concat_axis=0, axis_index_groups=[order], tiled=True
    )

    chunks = longitudes // CHUNK
    height = chunks * few_levels
    field = grid_field.reshape(2, band_rows, few_levels, chunks, CHUNK).transpose(0, 1, 3, 2, 4)
    field = field.reshape(2, band_rows, height, CHUNK)
    own_spec = pl.BlockSpec((1, slots), lambda g, *_: (0, 0))
    regroup_scratch = [
        pltpu.VMEM((slots // 128, 8, 128, 128), jnp.float32),
        pltpu.VMEM((slots // 128, 8, 128, 128), jnp.float32),
    ]

    far = pl.BlockSpec(memory_space=pltpu.HBM)
    made_shape = (16 * levels, 4 * levels)

    def matrix_spec(shape):
        return pl.BlockSpec(shape, lambda g, *_: (0, 0))

    def blocks_spec(height):
        return pl.BlockSpec((slots // 2, height, 128), lambda g, *_: (0, 0, 0))

    sums, phasors = pl.pallas_call(
        functools.partial(analysis_kernel, order),
        grid_spec=pltpu.PrefetchScalarGridSpec(
            num_scalar_prefetch=3,
            grid=(1,),
            in_specs=[
                own_spec,
                pl.BlockSpec((spectral_variance.shape[0], 128), lambda g, p, w, wave: (0, wave[0] // 2)),
                far,
            ],
            out_specs=[blocks_spec(24), far],
            scratch_shapes=[
                pltpu.VMEM(field.shape, jnp.bfloat16),
                pltpu.VMEM((15, band_rows, slots), jnp.float32),
                pltpu.VMEM((ROWS, CHUNK, 2 * slots), jnp.bfloat16),
                pltpu.VMEM((2, ROWS, 8, slots), jnp.float32),
            ] + regroup_scratch + [
                pltpu.SemaphoreType.DMA((band_rows // ROWS,)),
                pltpu.SemaphoreType.DMA((band_rows // ROWS,)),
            ],
        ),
        out_shape=[
            jax.ShapeDtypeStruct((slots // 2, 24, 128), jnp.bfloat16),
            jax.ShapeDtypeStruct((15, band_rows, slots), jnp.float32),
        ],
        compiler_params=params,
        name="analysis",
    )(points, weights, wave.reshape(1), own, spectral_variance, field)

    arrived = exchange(sums)

    phasors_spec = pl.BlockSpec((15, band_rows, slots), lambda g, *_: (0, 0, 0))
    table_shape = (band_rows // 2 - NEAR * (ROWS // 2), 2 * slots, 2 * CHUNK)
    near_shape = (NEAR * (ROWS // 2), 2 * slots, 2 * CHUNK)
    table, near_table, made = pl.pallas_call(
        table_kernel,
        grid=(1,),
        in_specs=[phasors_spec, matrix_spec((levels, levels))],
        out_specs=[far, pl.BlockSpec(near_shape, lambda g, *_: (0, 0, 0)), matrix_spec(made_shape)],
        scratch_shapes=[
            pltpu.VMEM(table_shape, jnp.bfloat16),
            pltpu.VMEM((ROWS, CHUNK, 2 * slots), jnp.bfloat16),
            pltpu.SemaphoreType.DMA((band_rows // ROWS - NEAR,)),
        ],
        out_shape=[
            jax.ShapeDtypeStruct(table_shape, jnp.bfloat16),
            jax.ShapeDtypeStruct(near_shape, jnp.bfloat16),
            jax.ShapeDtypeStruct(made_shape, jnp.bfloat16),
        ],
        compiler_params=pltpu.CompilerParams(vmem_limit_bytes=50 * 1024 * 1024),
        cost_estimate=pl.CostEstimate(flops=8 * 10**9, bytes_accessed=9 * 10**6, transcendentals=0),
        name="tables",
    )(phasors, vertical)

    remixed = pl.pallas_call(
        functools.partial(spectral_kernel, order),
        grid_spec=pltpu.PrefetchScalarGridSpec(
            num_scalar_prefetch=1,
            grid=(1,),
            in_specs=[blocks_spec(24), far, matrix_spec(made_shape)],
            out_specs=blocks_spec(16),
            scratch_shapes=[
                pltpu.VMEM((4, 2 * levels, rows), jnp.bfloat16),
                pltpu.VMEM((4, 2 * levels, rows), jnp.float32),
                pltpu.VMEM((2, 2, half_degree, rows), jnp.bfloat16),
                pltpu.SemaphoreType.DMA((2, 2)),
            ],
        ),
        out_shape=jax.ShapeDtypeStruct((slots // 2, 16, 128), jnp.bfloat16),
        compiler_params=pltpu.CompilerParams(vmem_limit_bytes=50 * 1024 * 1024),
        name="spectral",
    )(place, arrived, legendre, made)

    returned = exchange(remixed)

    smoothed = pl.pallas_call(
        functools.partial(synthesis_kernel, order),
        grid_spec=pltpu.PrefetchScalarGridSpec(
            num_scalar_prefetch=1,
            grid=(1,),
            in_specs=[own_spec, blocks_spec(16), far, pl.BlockSpec(memory_space=pl.ANY), phasors_spec],
            out_specs=far,
            scratch_shapes=[
                pltpu.VMEM(field.shape, jnp.bfloat16),
                pltpu.VMEM((band_rows // 2, 2 * slots, 2 * CHUNK), jnp.bfloat16),
                pltpu.VMEM((slots // 128, 8, 128, 128), jnp.float32),
                pltpu.VMEM((slots // 128, 128, 8, 128), jnp.float32),
                pltpu.SemaphoreType.DMA((band_rows // ROWS,)),
                pltpu.SemaphoreType.DMA((band_rows // ROWS,)),
            ],
        ),
        out_shape=jax.ShapeDtypeStruct(field.shape, jnp.bfloat16),
        compiler_params=pltpu.CompilerParams(vmem_limit_bytes=50 * 1024 * 1024),
        name="synthesis",
    )(points, own, returned, table, near_table, phasors)
    smoothed = smoothed.reshape(2, band_rows, chunks, few_levels, CHUNK).transpose(0, 1, 3, 2, 4)
    return smoothed.reshape(grid_field.shape)


def solution(mesh):
    return jax.shard_map(
        local,
        mesh=mesh,
        in_specs=(
            P(None, "lat", "wave", None),
            P("lat"),
            P("lat"),
            P(),
            P("wave", None, None, None),
            P("lat", None),
            P(),
        ),
        out_specs=P(None, "lat", "wave", None),
        check_vma=False,
    )
```

```python
import functools

import jax
import jax.numpy as jnp
from jax import lax
from jax.experimental import pallas as pl
from jax.experimental.pallas import tpu as pltpu
from jax.sharding import PartitionSpec as P

ROWS = 8
CHUNK = 128
NEAR = 2
VMEM_LIMIT = 56 * 1024 * 1024

SIN_TERMS = (3.141592640130707, -5.167710083507862, 2.550077523214134, -0.5982912856178576, 0.0776576603009221)
COS_TERMS = (0.9999999532476082, -4.93479283061961, 4.058411352862034, -1.3318765680776314, 0.2196896110917421)


def polynomial(terms, square):
    total = jnp.full_like(square, terms[-1])
    for term in terms[-2::-1]:
        total = total * square + term
    return total


def phasor(product, length, inverse):
    turns = jnp.floor(product * inverse + 0.5)
    part = (product - turns * length) * inverse
    square = part * part
    sine = part * polynomial(SIN_TERMS, square)
    cosine = polynomial(COS_TERMS, square)
    return 1.0 - 2.0 * sine * sine, 2.0 * sine * cosine


def multiply(a, b):
    return a[0] * b[0] - a[1] * b[1], a[0] * b[1] + a[1] * b[0]


def square(a):
    return a[0] * a[0] - a[1] * a[1], 2.0 * a[0] * a[1]


def times_transposed(a, b):
    return lax.dot_general(a, b, (((1,), (1,)), ((), ())), preferred_element_type=jnp.float32)


def lengths_by_row(points_ref, first, shape):
    row = lax.broadcasted_iota(jnp.int32, shape, 0)
    lengths = jnp.zeros(shape, jnp.int32)
    for r in range(ROWS):
        lengths = jnp.where(row == r, points_ref[first + r], lengths)
    lengths = lengths.astype(jnp.float32)
    return lengths, 1.0 / lengths


def place_phasors(step_ref, waves, lengths, inverse):
    cosine, sine = phasor(waves, lengths, inverse)
    turn, at = (cosine, -sine), 1
    keep = {1: 0, 2: 2, 4: 4, 8: 6, CHUNK: 10, 2 * CHUNK: 12}
    while True:
        if at in keep:
            step_ref[keep[at]], step_ref[keep[at] + 1] = turn
        if at in (8, 16, 2 * CHUNK):
            step_ref[{8: 8, 16: 9, 2 * CHUNK: 14}[at]] = 2.0 * turn[0]
        if at == 2 * CHUNK:
            break
        turn, at = square(turn), 2 * at


def swap_sublanes(values):
    values = list(values)
    sublane = lax.broadcasted_iota(jnp.int32, values[0].shape, 0)
    for d in (4, 2, 1):
        low = sublane & d == 0
        for a in range(8):
            if a & d == 0:
                first, second = values[a], values[a + d]
                values[a] = jnp.where(low, first, pltpu.roll(second, d, 0))
                values[a + d] = jnp.where(low, pltpu.roll(first, 8 - d, 0), second)
    return values


def steps_of(step_ref, which, r):
    slots = step_ref.shape[2]
    return tuple(jnp.broadcast_to(step_ref[n, r:r + 1, :], (8, slots)) for n in which)


def build_table(table_ref, step_ref, r):
    slots = step_ref.shape[2]
    size = table_ref.shape[0]
    sublane = lax.broadcasted_iota(jnp.int32, (8, slots), 0)
    powers = []
    for n in range(3):
        power = steps_of(step_ref, (2 * n, 2 * n + 1), r)
        powers.append(tuple(jnp.where(sublane & (1 << n) == 0, 1.0 - c, power[c]) for c in range(2)))
    real, imaginary, twice, twice_next = steps_of(step_ref, (6, 7, 8, 9), r)
    values = [multiply(multiply(powers[0], powers[1]), powers[2])]
    values.append(multiply(values[0], (real, imaginary)))
    for n in range(2, size // 8):
        if n < 4:
            values.append(tuple(twice * values[n - 1][c] - values[n - 2][c] for c in range(2)))
        else:
            values.append(tuple(twice_next * values[n - 2][c] - values[n - 4][c] for c in range(2)))
        if n % 2:
            for c in range(2):
                both = jnp.concatenate([values[n - 1][c], values[n][c]], axis=0).astype(jnp.bfloat16)
                table_ref[8 * n - 8:8 * n + 8, c * slots:(c + 1) * slots] = both
        elif n == 2:
            for c in range(2):
                both = jnp.concatenate([values[0][c], values[1][c]], axis=0).astype(jnp.bfloat16)
                table_ref[:16, c * slots:(c + 1) * slots] = both


def analysis_kernel(order, points_ref, weights_ref, wave_ref, owners_ref, variance_ref, field_ref, out_ref,
                    phasors_ref, own_ref, step_ref, table_ref, rows_ref, sums_ref, order_ref, sems, phasor_sems):
    slots = owners_ref.shape[1]
    tiles = [slice(t, t + 128) for t in range(0, slots, 128)]
    rows, height = own_ref.shape[1:3]

    def arrival(g):
        at = pl.ds(g * ROWS, ROWS)
        return pltpu.make_async_copy(field_ref.at[:, at], own_ref.at[:, at], sems.at[g])

    def departure(g):
        at = pl.ds(pl.multiple_of(g * ROWS, ROWS), ROWS)
        return pltpu.make_async_copy(step_ref.at[:, at], phasors_ref.at[:, at], phasor_sems.at[g])

    for g in range(rows // ROWS):
        arrival(g).start()
    waves = jnp.broadcast_to(owners_ref[...].astype(jnp.float32), (ROWS, slots))
    sublane = lax.broadcasted_iota(jnp.int32, (8, slots), 0)
    position = lax.broadcasted_iota(jnp.int32, (height, CHUNK), 0) // 4 * CHUNK
    position = position + lax.broadcasted_iota(jnp.int32, (height, CHUNK), 1)

    def group(g, _):
        first = g * ROWS
        lengths, inverse = lengths_by_row(points_ref, first, (ROWS, slots))
        here = step_ref.at[:, pl.ds(pl.multiple_of(first, ROWS), ROWS)]
        place_phasors(here, waves, lengths, inverse)
        departure(g).start()
        arrival(g).wait()
        for r in range(ROWS):
            length = points_ref[first + r]

            build_table(table_ref.at[r], here, r)
            inside = jnp.where(position < length, 1.0, 0.0).astype(jnp.bfloat16)
            points = jnp.concatenate([own_ref[0, first + r] * inside, own_ref[1, first + r] * inside], axis=0)
            parts = jnp.dot(points, table_ref[r], preferred_element_type=jnp.float32)
            chunk, pair, twice = steps_of(here, (10, 11), r), steps_of(here, (12, 13), r), steps_of(here, (14,), r)[0]
            sums = []
            for h in range(2):
                blocks = [
                    tuple(parts[b:b + 8, c * slots:(c + 1) * slots] for c in range(2))
                    for b in range(h * height, (h + 1) * height, 8)
                ]
                later, total = blocks[-1], tuple(blocks[-2][c] + twice * blocks[-1][c] for c in range(2))
                for part in blocks[-3:0:-1]:
                    later, total = total, tuple(part[c] + (twice * total[c] - later[c]) for c in range(2))
                total = multiply(total, pair)
                sums.append(tuple(total[c] + (blocks[0][c] - later[c]) for c in range(2)))
            scale = weights_ref[first + r] / length.astype(jnp.float32)
            scale = jnp.where(2 * owners_ref[...] < length, scale, 0.0)
            firsts, seconds = [], []
            for c in range(2):
                added, taken = sums[0][c] + sums[1][c], sums[0][c] - sums[1][c]
                firsts.append(jnp.where(sublane < 4, added, pltpu.roll(taken, 4, 0)))
                seconds.append(jnp.where(sublane < 4, pltpu.roll(added, 4, 0), taken))
            seconds = multiply(seconds, chunk)
            for c in range(2):
                rows_ref[c, r] = (firsts[c] + seconds[c]) * scale
        for c in range(2):
            for t, lanes in enumerate(tiles):
                for row, part in enumerate(swap_sublanes([rows_ref[c, r, :, lanes] for r in range(ROWS)])):
                    sums_ref[t, row, pl.ds(pl.multiple_of(c * 64 + first, 8), 8), :] = part
        return 0

    lax.fori_loop(0, rows // ROWS, group, 0)

    for row in range(8):
        for t in range(len(tiles)):
            order_ref[t, row] = sums_ref[t, row].T
    variance = variance_ref[...]
    variance = jnp.where(wave_ref[0] % 2 == 1, pltpu.roll(variance, 64, 1), variance)
    upper = variance.astype(jnp.bfloat16).astype(jnp.float32)
    lane = lax.broadcasted_iota(jnp.int32, variance.shape, 1)
    variance = jnp.where(lane < 64, upper, pltpu.roll(variance - upper, 64, 1)).astype(jnp.bfloat16)
    where = {t: n for n, t in enumerate(order)}
    for slot in range(0, slots, 8):
        at = slice(slot % 128, slot % 128 + 8)
        parts = swap_sublanes([order_ref[slot // 128, row, at, :] for row in range(8)])
        for n in range(0, 8, 2):
            to = where[(slot + n) // 2]
            out_ref[to, :16] = jnp.concatenate(parts[n:n + 2], axis=0).astype(jnp.bfloat16)
            out_ref[to, 16:] = variance
    for g in range(rows // ROWS):
        departure(g).wait()


def matrices_of(made_ref):
    size = made_ref.shape[1]
    return made_ref.at[:size], made_ref.at[size:2 * size], made_ref.at[2 * size:]


def place_matrices(vertical_ref, mix_in_ref, mix_out_ref, parting_ref):
    levels = vertical_ref.shape[0]
    vertical = vertical_ref[...].astype(jnp.float32)
    index = lax.broadcasted_iota(jnp.int32, (4 * levels, levels), 0)
    level = lax.broadcasted_iota(jnp.int32, (4 * levels, levels), 1)
    by_block = jnp.where(level == index // 16 * 4 + index % 4, 1.0, 0.0)
    by_slot = jnp.where(level == index % levels, 1.0, 0.0)
    row = lax.broadcasted_iota(jnp.int32, (4 * levels, 4 * levels), 0)
    col = lax.broadcasted_iota(jnp.int32, (4 * levels, 4 * levels), 1)
    by_rows = jnp.dot(by_block, vertical, preferred_element_type=jnp.float32)
    mix_in = times_transposed(by_slot, by_rows)
    mix_in_ref[...] = jnp.where(row // levels == col % 16 // 4, mix_in, 0.0).astype(jnp.bfloat16)
    mix_out = times_transposed(by_rows, by_slot)
    sign = jnp.where((row % 8 // 4 == 1) & (col // levels % 2 == 1), -1.0, 1.0)
    mix_out_ref[...] = jnp.where(row % 16 // 8 == col // (2 * levels), mix_out * sign, 0.0).astype(jnp.bfloat16)
    degree = lax.broadcasted_iota(jnp.int32, parting_ref.shape, 0)
    degree = degree // 128 * 64 + degree % 64
    lane = lax.broadcasted_iota(jnp.int32, parting_ref.shape, 1)
    parting_ref[...] = jnp.where(degree == 2 * (lane % 128) + lane // 128, 1.0, 0.0).astype(jnp.bfloat16)


def table_kernel(step_ref, vertical_ref, out_ref, near_ref, made_ref, pairs_ref, table_ref, sems):
    groups = step_ref.shape[1] // ROWS - NEAR

    def departure(g):
        at = pl.ds(g * (ROWS // 2), ROWS // 2)
        return pltpu.make_async_copy(pairs_ref.at[at], out_ref.at[at], sems.at[g])

    def group(g, to_ref, at):
        here = step_ref.at[:, pl.ds(pl.multiple_of(g * ROWS, ROWS), ROWS)]
        for r in range(ROWS):
            build_table(table_ref.at[r], here, r)
            to_ref[at * (ROWS // 2) + r // 2, :, (r % 2) * CHUNK:(r % 2 + 1) * CHUNK] = table_ref[r].T

    def far_group(g, _):
        group(g + NEAR, pairs_ref, g)
        departure(g).start()
        return 0

    lax.fori_loop(0, groups, far_group, 0)
    lax.fori_loop(0, NEAR, lambda g, _: (group(g, near_ref, g), 0)[1], 0)
    place_matrices(vertical_ref, *matrices_of(made_ref))
    for g in range(groups):
        departure(g).wait()


def synthesis_kernel(order, points_ref, owners_ref, values_ref, far_table_ref, near_table_ref, turns_ref, out_ref,
                     own_ref, table_ref, order_ref, coefs_ref, table_sems, sems):
    slots = owners_ref.shape[1]
    tiles = [slice(t, t + 128) for t in range(0, slots, 128)]
    rows, height = own_ref.shape[1:3]

    def arrival(g, near):
        to = table_ref.at[pl.ds(g * (ROWS // 2), ROWS // 2)]
        at = pl.ds((g if near else g - NEAR) * (ROWS // 2), ROWS // 2)
        return pltpu.make_async_copy((near_table_ref if near else far_table_ref).at[at], to, table_sems.at[g])

    def departure(g):
        at = pl.ds(g * ROWS, ROWS)
        return pltpu.make_async_copy(own_ref.at[:, at], out_ref.at[:, at], sems.at[g])

    for g in range(rows // ROWS):
        arrival(g, g < NEAR).start()
    where = {t: n for n, t in enumerate(order)}
    for slot in range(0, slots, 8):
        parts = []
        for n in range(0, 8, 2):
            pair = values_ref[where[(slot + n) // 2]].astype(jnp.float32)
            parts += [pair[:8], pair[8:]]
        for row, part in enumerate(swap_sublanes(parts)):
            order_ref[slot // 128, row, slot % 128:slot % 128 + 8, :] = part
    for t in range(len(tiles)):
        for row in range(8):
            order_ref[t, row] = order_ref[t, row].T
        for n in range(0, 128, 8):
            parts = swap_sublanes([order_ref[t, row, n:n + 8, :] for row in range(8)])
            for at, part in enumerate(parts):
                coefs_ref[t, n + at] = part

    doubling = jnp.where(owners_ref[...] == 0, 1.0, 2.0)
    sublane = lax.broadcasted_iota(jnp.int32, (8, slots), 0)
    position = lax.broadcasted_iota(jnp.int32, (height, CHUNK), 0) // 4 * CHUNK
    position = position + lax.broadcasted_iota(jnp.int32, (height, CHUNK), 1)

    def group(g, near):
        first = g * ROWS
        arrival(g, near).wait()
        for r in range(ROWS):
            row = first + r
            length = points_ref[row]
            turns = [jnp.broadcast_to(turns_ref[n, pl.ds(row, 1), :], (8, slots)) for n in range(10, 15)]
            chunk, pair, twice = (turns[0], -turns[1]), (turns[2], -turns[3]), turns[4]
            scale = jnp.where(2 * owners_ref[...] < length, doubling, 0.0)
            start = tuple(jnp.where(sublane < 4, 1.0 - c, chunk[c]) * scale for c in range(2))
            values = [
                [coefs_ref[t, c * 64 + row] for t in range(len(tiles))]
                for c in range(2)
            ]
            values = [jnp.concatenate(part, axis=1) for part in values]
            others = [pltpu.roll(part, 4, 0) for part in values]
            turned = []
            for low, high in ((values, others), (others, values)):
                before = multiply(start, [jnp.where(sublane < 4, low[c], high[c]) for c in range(2)])
                value = multiply(before, pair)
                turned += [jnp.concatenate(before, axis=1), jnp.concatenate(value, axis=1)]
                for _ in range(2, height // 8):
                    before, value = value, tuple(twice * value[c] - before[c] for c in range(2))
                    turned.append(jnp.concatenate(value, axis=1))
            turned = jnp.concatenate(turned, axis=0).astype(jnp.bfloat16)
            table = table_ref[g * (ROWS // 2) + r // 2, :, (r % 2) * CHUNK:(r % 2 + 1) * CHUNK]
            gridded = jnp.dot(turned, table, preferred_element_type=jnp.float32)
            for h in range(2):
                own_ref[h, row] = jnp.where(
                    position < length, gridded[h * height:(h + 1) * height], 0.0
                ).astype(jnp.bfloat16)
        departure(g).start()

    for start, end, near in ((0, NEAR, True), (NEAR, rows // ROWS, False)):
        lax.fori_loop(start, end, lambda g, _, near=near: (group(g, near), 0)[1], 0)
    for g in range(rows // ROWS):
        departure(g).wait()


def swap_halves(first, second):
    low = lax.broadcasted_iota(jnp.int32, first.shape, 1) < 64
    return (
        jnp.where(low, first, pltpu.roll(second, 64, 1)),
        jnp.where(low, pltpu.roll(first, 64, 1), second),
    )


def spectral_kernel(order, place_ref, values_ref, legendre_ref, made_ref, out_ref,
                    mixed_ref, back_ref, own_ref, sems):
    levels = made_ref.shape[1] // 4
    copies = {}
    for slot in range(2):
        for q in range(2):
            copies[slot, q] = pltpu.make_async_copy(
                legendre_ref.at[place_ref[0] + slot, q], own_ref.at[slot, q], sems.at[slot, q]
            )
            copies[slot, q].start()
    mix_in, mix_out, parting = (part[...] for part in matrices_of(made_ref))
    where = {t: n for n, t in enumerate(order)}
    for p in range(4):
        bands = [
            jnp.concatenate([values_ref[where[w * 8 + v], :16] for w in range(16)], axis=0)
            for v in (2 * p, 2 * p + 1)
        ]
        mixed = jnp.dot(mix_in, jnp.concatenate(bands, axis=1), preferred_element_type=jnp.float32)
        for c, part in enumerate(swap_halves(mixed[:, :128], mixed[:, 128:])):
            part = part.astype(jnp.bfloat16)
            for k in range(4):
                mixed_ref[k, c * levels:(c + 1) * levels, p * 128:(p + 1) * 128] = (
                    part[k * levels:(k + 1) * levels]
                )
    halves = [
        jnp.concatenate([values_ref[where[w * 8 + v], 16:].astype(jnp.float32) for v in range(8)], axis=0)
        for w in range(16)
    ]
    halves = jnp.concatenate([jnp.concatenate(halves[n:n + 4], axis=1) for n in range(0, 16, 4)], axis=0)
    parted = jnp.dot(halves.astype(jnp.bfloat16), parting, preferred_element_type=jnp.float32)
    parted = [parted[n * levels:(n + 1) * levels] for n in range(4)]
    spreads = [jnp.concatenate([part[:, q * 128:(q + 1) * 128] for part in parted], axis=1) for q in range(2)]
    for slot in range(2):
        parity = place_ref[1 + slot]
        for q in range(2):
            s = (q + parity) % 2
            copies[slot, q].wait()
            values = own_ref[slot, q]
            coefficient = times_transposed(mixed_ref[2 * slot + s], values)
            spread = spreads[q]
            scaled = coefficient * jnp.concatenate([spread, spread], axis=0)
            back_ref[2 * slot + s] = jnp.dot(
                scaled.astype(jnp.bfloat16), values, preferred_element_type=jnp.float32
            )
    for p in range(4):
        lanes = slice(p * 128, (p + 1) * 128)
        halves = [
            jnp.concatenate([back_ref[k, c * levels:(c + 1) * levels, lanes] for k in range(4)], axis=0)
            for c in range(2)
        ]
        parts = jnp.concatenate(swap_halves(*halves), axis=1).astype(jnp.bfloat16)
        remixed = jnp.dot(mix_out, parts, preferred_element_type=jnp.float32).astype(jnp.bfloat16)
        for n in range(2):
            for w in range(16):
                out_ref[where[w * 8 + 2 * p + n]] = remixed[16 * w:16 * w + 16, n * 128:(n + 1) * 128]


def local(grid_field, points, weights, owners, legendre, spectral_variance, vertical):
    _, band_rows, few_levels, longitudes = grid_field.shape
    slots = owners.shape[0]
    levels = vertical.shape[0]
    half_degree, rows = legendre.shape[2:]
    wave, lat = lax.axis_index("wave"), lax.axis_index("lat")
    own = owners.reshape(1, slots)
    parities = lax.dynamic_slice_in_dim(owners, 2 * (wave * lax.axis_size("lat") + lat), 2, 0) % 2
    place = jnp.concatenate([(2 * lat).reshape(1), parities])
    params = pltpu.CompilerParams(vmem_limit_bytes=VMEM_LIMIT)

    order = [37 * t % (slots // 2) for t in range(slots // 2)]
    exchange = functools.partial(
        lax.all_to_all, axis_name=("wave", "lat"), split_axis=0, concat_axis=0, axis_index_groups=[order], tiled=True
    )

    chunks = longitudes // CHUNK
    height = chunks * few_levels
    field = grid_field.reshape(2, band_rows, few_levels, chunks, CHUNK).transpose(0, 1, 3, 2, 4)
    field = field.reshape(2, band_rows, height, CHUNK)
    own_spec = pl.BlockSpec((1, slots), lambda g, *_: (0, 0))
    regroup_scratch = [
        pltpu.VMEM((slots // 128, 8, 128, 128), jnp.float32),
        pltpu.VMEM((slots // 128, 8, 128, 128), jnp.float32),
    ]

    far = pl.BlockSpec(memory_space=pltpu.HBM)
    made_shape = (16 * levels, 4 * levels)

    def matrix_spec(shape):
        return pl.BlockSpec(shape, lambda g, *_: (0, 0))

    def blocks_spec(height):
        return pl.BlockSpec((slots // 2, height, 128), lambda g, *_: (0, 0, 0))

    sums, phasors = pl.pallas_call(
        functools.partial(analysis_kernel, order),
        grid_spec=pltpu.PrefetchScalarGridSpec(
            num_scalar_prefetch=3,
            grid=(1,),
            in_specs=[
                own_spec,
                pl.BlockSpec((spectral_variance.shape[0], 128), lambda g, p, w, wave: (0, wave[0] // 2)),
                far,
            ],
            out_specs=[blocks_spec(24), far],
            scratch_shapes=[
                pltpu.VMEM(field.shape, jnp.bfloat16),
                pltpu.VMEM((15, band_rows, slots), jnp.float32),
                pltpu.VMEM((ROWS, CHUNK, 2 * slots), jnp.bfloat16),
                pltpu.VMEM((2, ROWS, 8, slots), jnp.float32),
            ] + regroup_scratch + [
                pltpu.SemaphoreType.DMA((band_rows // ROWS,)),
                pltpu.SemaphoreType.DMA((band_rows // ROWS,)),
            ],
        ),
        out_shape=[
            jax.ShapeDtypeStruct((slots // 2, 24, 128), jnp.bfloat16),
            jax.ShapeDtypeStruct((15, band_rows, slots), jnp.float32),
        ],
        compiler_params=params,
        name="analysis",
    )(points, weights, wave.reshape(1), own, spectral_variance, field)

    arrived = exchange(sums)

    phasors_spec = pl.BlockSpec((15, band_rows, slots), lambda g, *_: (0, 0, 0))
    table_shape = (band_rows // 2 - NEAR * (ROWS // 2), 2 * slots, 2 * CHUNK)
    near_shape = (NEAR * (ROWS // 2), 2 * slots, 2 * CHUNK)
    table, near_table, made = pl.pallas_call(
        table_kernel,
        grid=(1,),
        in_specs=[phasors_spec, matrix_spec((levels, levels))],
        out_specs=[far, pl.BlockSpec(near_shape, lambda g, *_: (0, 0, 0)), matrix_spec(made_shape)],
        scratch_shapes=[
            pltpu.VMEM(table_shape, jnp.bfloat16),
            pltpu.VMEM((ROWS, CHUNK, 2 * slots), jnp.bfloat16),
            pltpu.SemaphoreType.DMA((band_rows // ROWS - NEAR,)),
        ],
        out_shape=[
            jax.ShapeDtypeStruct(table_shape, jnp.bfloat16),
            jax.ShapeDtypeStruct(near_shape, jnp.bfloat16),
            jax.ShapeDtypeStruct(made_shape, jnp.bfloat16),
        ],
        compiler_params=pltpu.CompilerParams(vmem_limit_bytes=50 * 1024 * 1024),
        cost_estimate=pl.CostEstimate(flops=8 * 10**9, bytes_accessed=9 * 10**6, transcendentals=0),
        name="tables",
    )(phasors, vertical)

    remixed = pl.pallas_call(
        functools.partial(spectral_kernel, order),
        grid_spec=pltpu.PrefetchScalarGridSpec(
            num_scalar_prefetch=1,
            grid=(1,),
            in_specs=[blocks_spec(24), far, matrix_spec(made_shape)],
            out_specs=blocks_spec(16),
            scratch_shapes=[
                pltpu.VMEM((4, 2 * levels, rows), jnp.bfloat16),
                pltpu.VMEM((4, 2 * levels, rows), jnp.float32),
                pltpu.VMEM((2, 2, half_degree, rows), jnp.bfloat16),
                pltpu.SemaphoreType.DMA((2, 2)),
            ],
        ),
        out_shape=jax.ShapeDtypeStruct((slots // 2, 16, 128), jnp.bfloat16),
        compiler_params=pltpu.CompilerParams(vmem_limit_bytes=50 * 1024 * 1024),
        name="spectral",
    )(place, arrived, legendre, made)

    returned = exchange(remixed)

    smoothed = pl.pallas_call(
        functools.partial(synthesis_kernel, order),
        grid_spec=pltpu.PrefetchScalarGridSpec(
            num_scalar_prefetch=1,
            grid=(1,),
            in_specs=[own_spec, blocks_spec(16), far, pl.BlockSpec(memory_space=pl.ANY), phasors_spec],
            out_specs=far,
            scratch_shapes=[
                pltpu.VMEM(field.shape, jnp.bfloat16),
                pltpu.VMEM((band_rows // 2, 2 * slots, 2 * CHUNK), jnp.bfloat16),
                pltpu.VMEM((slots // 128, 8, 128, 128), jnp.float32),
                pltpu.VMEM((slots // 128, 128, 8, 128), jnp.float32),
                pltpu.SemaphoreType.DMA((band_rows // ROWS,)),
                pltpu.SemaphoreType.DMA((band_rows // ROWS,)),
            ],
        ),
        out_shape=jax.ShapeDtypeStruct(field.shape, jnp.bfloat16),
        compiler_params=pltpu.CompilerParams(vmem_limit_bytes=50 * 1024 * 1024),
        name="synthesis",
    )(points, own, returned, table, near_table, phasors)
    smoothed = smoothed.reshape(2, band_rows, chunks, few_levels, CHUNK).transpose(0, 1, 3, 2, 4)
    return smoothed.reshape(grid_field.shape)


def solution(mesh):
    return jax.shard_map(
        local,
        mesh=mesh,
        in_specs=(
            P(None, "lat", "wave", None),
            P("lat"),
            P("lat"),
            P(),
            P("wave", None, None, None),
            P("lat", None),
            P(),
        ),
        out_specs=P(None, "lat", "wave", None),
        check_vma=False,
    )
```
